128 devices in a mesh: section: 2 (over core), expert: 16 (over y, z), dp: 4 (over x).
Axes of the slice: x: 4, y: 4, z: 4, core: 2. Of those that a mesh axis runs over, the one named last changes fastest.
Arguments:
- section_ends: bfloat16 [2, 16384, 768], P('section', ('expert', 'dp')), may hold values from -12 to 12
- routes: int32 [2, 16384, 1], P('section', ('expert', 'dp')), may hold values from 0 to 15, as said below
- query_weight: bfloat16 [2, 768, 768], P('section'), may hold values from -0.21875 to 0.21875
- key_weight: bfloat16 [2, 768, 768], P('section'), may hold values from -0.21875 to 0.21875
- value_weight: bfloat16 [2, 768, 768], P('section'), may hold values from -0.21875 to 0.21875
- out_weight: bfloat16 [2, 768, 768], P('section'), may hold values from -0.625 to 0.625
- query_bias: float32 [2, 768], P('section'), may hold values from -2 to 2
- value_bias: float32 [2, 768], P('section'), may hold values from -2 to 2
- out_bias: float32 [2, 768], P('section'), may hold values from -2 to 2
- attention_gain: float32 [2, 768], P('section'), may hold values from 0.1 to 1.9
- mixture_gain: float32 [2, 768], P('section'), may hold values from 0.1 to 1.9
- router_weight: bfloat16 [2, 768, 16], P('section'), may hold values from -0.15625 to 0.15625
- expert_in: bfloat16 [2, 16, 768, 3072], P('section', 'expert', None, 'dp'), may hold values from -0.21875 to 0.21875
- expert_down: bfloat16 [2, 16, 3072, 768], P('section', 'expert', 'dp'), may hold values from -1.75 to 1.75
Outputs:
- activations: bfloat16 [2, 16384, 768], P('section', ('expert', 'dp'))
- input_grads: bfloat16 [2, 16384, 768], P('section', ('expert', 'dp'))
- balance: float32 [2, 2], P('section')
- query_grad: float32 [2, 768, 768], P('section')
- key_grad: float32 [2, 768, 768], P('section')
- value_grad: float32 [2, 768, 768], P('section')
- out_grad: float32 [2, 768, 768], P('section')
- query_bias_grad: float32 [2, 768], P('section')
- value_bias_grad: float32 [2, 768], P('section')
- out_bias_grad: float32 [2, 768], P('section')
- attention_gain_grad: float32 [2, 768], P('section')
- mixture_gain_grad: float32 [2, 768], P('section')
- router_grad: float32 [2, 768, 16], P('section')
- expert_in_grad: float32 [2, 16, 768, 3072], P('section', 'expert', None, 'dp')
- expert_down_grad: float32 [2, 16, 3072, 768], P('section', 'expert', 'dp')
The draws below stay inside these ranges and needn't reach their ends.
Inputs may be any that keep to these rules, and one draw needn't show every extreme that they name: `routes`: in each aligned block of 128 rows (one group's tokens in one micro-batch of one layer), no expert is named by more than 12 rows, and some expert is named by exactly 12 rows in every block.
All inputs are finite; a program needn't handle non-finite values.
Results may differ from the reference program's by a relative error of at most 0.0095.
Values may be sent and summed in bfloat16 or wider, within the bound.
No kernel may reach another device: no remote copies, remote signals or barrier semaphores. Data moves between devices by JAX's collectives and lax.ppermute only.
A program may use at most 192 MiB of HBM per device.

```python
import jax
import jax.numpy as jnp
from jax import lax

D = 768
HEADS = 12
HEAD_DIM = 64
FF = 3072
SEQ = 128
MICRO = 2
EXPERTS = 16
ROWS = 128
CAP = 12
GROUPS = 64
TOKENS = 16384
N_SECTION = 2


def draw_routes(key, part):
    key = jax.random.fold_in(key, 11)
    offset_key, order_key = jax.random.split(key)
    group_ids = jnp.arange(GROUPS, dtype=jnp.int32)
    leading = group_ids * group_ids * EXPERTS // (GROUPS * GROUPS)
    offsets = jax.random.randint(offset_key, (N_SECTION,), 0, EXPERTS, dtype=jnp.int32)
    row_ids = jnp.arange(ROWS, dtype=jnp.int32)
    filled = ROWS // CAP
    window = jnp.where(row_ids < filled * CAP, row_ids // CAP, filled)
    chosen = (leading[None, :, None, None] + offsets[:, None, None, None] + window[None, None, None, :]) % EXPERTS
    chosen = jnp.broadcast_to(chosen, (N_SECTION, GROUPS, MICRO, ROWS))
    order_keys = jax.random.split(order_key, N_SECTION * GROUPS * MICRO)
    orders = jax.vmap(lambda single: jax.random.permutation(single, ROWS))(order_keys)
    orders = orders.reshape(N_SECTION, GROUPS, MICRO, ROWS).astype(jnp.int32)
    shuffled = jnp.take_along_axis(chosen, orders, axis=-1)
    return shuffled.reshape(N_SECTION, TOKENS, 1).astype(jnp.int32)


def draw_section_ends(key, part):
    key = jax.random.fold_in(key, 5)
    noise_key, common_key = jax.random.split(key, 2)
    group_of = jnp.arange(TOKENS, dtype=jnp.int32) // (MICRO * ROWS)
    rising = 0.5 + 1.5 * group_of.astype(jnp.float32) / (GROUPS - 1)
    common = jnp.clip(jax.random.normal(common_key, (N_SECTION, GROUPS, D), jnp.float32), -4.0, 4.0)
    noise = jnp.clip(jax.random.normal(noise_key, (N_SECTION, TOKENS, D), jnp.float32), -4.0, 4.0)
    mixed = (noise + rising[None, :, None] * common[:, group_of, :]) / jnp.sqrt(1.0 + rising * rising)[None, :, None]
    return mixed.astype(jnp.bfloat16)


def levels(stream_key, extent, cuts, low, high):
    def one(dim, shards_of):
        draws = jax.random.uniform(jax.random.fold_in(jax.random.fold_in(stream_key, 6), dim), (shards_of,), jnp.float32, low / len(cuts), high / len(cuts))
        return jnp.repeat(jnp.exp(draws), extent[dim] // shards_of).reshape((-1,) + (1,) * (len(extent) - dim - 1))

    gain = one(*cuts[0])
    for cut in cuts[1:]:
        gain = gain * one(*cut)
    return gain


def gaussian(own_key, extent, width, reach, cuts=(), kind=jnp.bfloat16):
    values = width * jax.random.normal(own_key, extent, jnp.float32)
    if cuts:
        values = values * levels(own_key, extent, cuts, -0.22, 0.18)
    return jnp.clip(values, -reach, reach).astype(kind)


def setup_inputs(seed: int = 0) -> dict:
    streams_of = jax.random.split(jax.random.key(seed), 15)
    section_ends = draw_section_ends(jax.random.fold_in(streams_of[14], 71), 0)
    routes = draw_routes(jax.random.fold_in(streams_of[14], 71), 0)
    query_weight = gaussian(streams_of[2], (N_SECTION, D, D), D ** -0.5, 0.21875, ((0, 2),))
    key_weight = gaussian(streams_of[3], (N_SECTION, D, D), D ** -0.5, 0.21875, ((0, 2),))
    value_weight = gaussian(streams_of[4], (N_SECTION, D, D), D ** -0.5, 0.21875, ((0, 2),))
    out_weight = gaussian(streams_of[5], (N_SECTION, D, D), (max(D * 16 // SEQ, 1)) ** -0.5, 0.625, ((0, 2),))
    query_bias = gaussian(streams_of[6], (N_SECTION, D), 0.3, 2.0, ((0, 2),), jnp.float32)
    value_bias = gaussian(streams_of[7], (N_SECTION, D), 0.3, 2.0, ((0, 2),), jnp.float32)
    out_bias = gaussian(streams_of[8], (N_SECTION, D), 0.3, 2.0, ((0, 2),), jnp.float32)
    attention_gain = jnp.clip(1.0 + 0.18 * jax.random.normal(streams_of[9], (N_SECTION, D), jnp.float32), 0.1, 1.9)
    mixture_gain = jnp.clip(1.0 + 0.18 * jax.random.normal(streams_of[10], (N_SECTION, D), jnp.float32), 0.1, 1.9)
    router_weight = gaussian(streams_of[11], (N_SECTION, D, EXPERTS), (2 * D) ** -0.5, 0.15625, ((0, 2),))
    expert_in = gaussian(streams_of[12], (N_SECTION, EXPERTS, D, FF), D ** -0.5, 0.21875, ((0, 2), (1, 16), (3, 4)))
    expert_down = gaussian(streams_of[13], (N_SECTION, EXPERTS, FF, D), (max(FF // (EXPERTS * EXPERTS), 1)) ** -0.5, 1.75, ((0, 2), (1, 16), (2, 4)))
    return {"section_ends": section_ends, "routes": routes, "query_weight": query_weight, "key_weight": key_weight, "value_weight": value_weight, "out_weight": out_weight, "query_bias": query_bias, "value_bias": value_bias, "out_bias": out_bias, "attention_gain": attention_gain, "mixture_gain": mixture_gain, "router_weight": router_weight, "expert_in": expert_in, "expert_down": expert_down}


@jax.custom_vjp
def low(v):
    return lax.optimization_barrier(v.astype(jnp.bfloat16)).astype(jnp.float32)

@jax.custom_vjp
def low_back(v):
    return v

def low_keep(v):
    return (low(v), None)

def low_pass(kept, grad):
    return (grad,)

def back_keep(v):
    return (v, None)

def back_low(kept, grad):
    return (low(grad),)
low.defvjp(low_keep, low_pass)
low_back.defvjp(back_keep, back_low)
balance_factor = 20.0
epsilon = 1e-06
highest = lax.Precision.HIGHEST

def rms_scale(tensor):
    return lax.rsqrt(lax.optimization_barrier(jnp.mean(tensor * tensor, axis=-1, keepdims=True)) + epsilon)

def matmul(left, right):
    return jnp.matmul(left, right, precision=highest)

def both_ways(tensor):
    return low(low_back(tensor))

def split_heads(tensor):
    return tensor.reshape(-1, SEQ, HEADS, HEAD_DIM)

def section_layer(inputs, params, route_ids):
    query_weight, key_weight, value_weight, out_weight, query_bias, value_bias, out_bias, attention_gain, mixture_gain, router_weight, expert_in, expert_down = params
    scaling = HEAD_DIM ** (-0.5)
    normed = low(inputs * rms_scale(inputs) * attention_gain)
    queries = both_ways(matmul(normed, query_weight) + query_bias)
    key_rows = both_ways(matmul(normed, key_weight))
    values = both_ways(matmul(normed, value_weight) + value_bias)
    scores = low_back(jnp.einsum('sqhd,skhd->shqk', split_heads(queries), split_heads(key_rows), precision=highest) * scaling)
    log_total = jax.nn.logsumexp(scores, axis=-1, keepdims=True)
    weights = low(jnp.exp(scores - log_total))
    attended = jnp.einsum('shqk,skhd->sqhd', weights, split_heads(values), precision=highest)
    attended = both_ways(attended.reshape(inputs.shape))
    hidden = inputs + low_back(matmul(attended, out_weight) + out_bias)
    normed_moe = low(hidden * rms_scale(hidden) * mixture_gain)
    router_probs = jax.nn.softmax(matmul(normed_moe, router_weight), axis=-1)
    onehot = (route_ids[..., None] == jnp.arange(EXPERTS, dtype=jnp.int32)).astype(jnp.float32)
    slot_rank = lax.optimization_barrier(jnp.sum((jnp.cumsum(onehot, axis=1) - 1.0) * onehot, axis=-1))
    slot_hot = (slot_rank[..., None] == jnp.arange(CAP, dtype=jnp.float32)).astype(jnp.float32)
    placing = onehot[..., :, None] * slot_hot[..., None, :]
    gating = lax.optimization_barrier(jnp.sum(router_probs * onehot, axis=-1))
    buffers = low_back(jnp.einsum('grec,grd->egcd', placing, normed_moe, precision=highest))
    pre_act = low_back(jnp.einsum('egcd,edf->egcf', buffers, expert_in, precision=highest))
    activated = low(jax.nn.gelu(pre_act))
    expert_result = both_ways(jnp.einsum('egcf,efd->egcd', activated, expert_down, precision=highest))
    combined = jnp.einsum('grec,egcd->grd', placing, expert_result, precision=highest)
    result = hidden + gating[..., None] * combined
    token_total = inputs.shape[0] * inputs.shape[1]
    fraction = lax.optimization_barrier(jnp.sum(onehot, axis=(0, 1))) / token_total
    prob_share = lax.optimization_barrier(jnp.sum(router_probs, axis=(0, 1))) / token_total
    balance = EXPERTS * jnp.sum(fraction * prob_share)
    return (low(result), balance)

def reference(section_ends, routes, query_weight, key_weight, value_weight, out_weight, query_bias, value_bias, out_bias, attention_gain, mixture_gain, router_weight, expert_in, expert_down):
    params = tuple((member.astype(jnp.float32) for member in (query_weight, key_weight, value_weight, out_weight, query_bias, value_bias, out_bias, attention_gain, mixture_gain, router_weight, expert_in, expert_down)))
    start = section_ends[0].astype(jnp.float32).reshape(GROUPS, MICRO, ROWS, D)
    cotangent = section_ends[1].astype(jnp.float32).reshape(GROUPS, MICRO, ROWS, D)
    route_ids = routes[:, :, 0].reshape(N_SECTION, GROUPS, MICRO, ROWS)

    def run_section(section_no, section_params, inputs):
        results = []
        balances = []
        for micro_no in range(MICRO):
            result, balance = section_layer(inputs[:, micro_no], section_params, route_ids[section_no, :, micro_no])
            results.append(result)
            balances.append(balance)
        return (jnp.stack(results, axis=1), jnp.stack(balances))

    def forward(params, inputs, probe_in):
        first_set = tuple((member[0] for member in params))
        second = tuple((member[1] for member in params))
        first_out, first_bal = run_section(0, first_set, inputs)
        second_out, second_bal = run_section(1, second, low_back(first_out) + probe_in)
        return (first_out, second_out, jnp.stack([first_bal, second_bal]))
    probe_in = jnp.zeros_like(start)
    (first_out, second_out, balance), pullback = jax.vjp(forward, params, start, probe_in)
    balance_weight = balance_factor * GROUPS * ROWS
    gradients, start_grad, probe_grad = pullback((jnp.zeros_like(first_out), cotangent, jnp.full_like(balance, balance_weight)))
    activations = jnp.stack([first_out, second_out]).reshape(N_SECTION, TOKENS, D).astype(jnp.bfloat16)
    input_grads = jnp.stack([start_grad, probe_grad]).reshape(N_SECTION, TOKENS, D).astype(jnp.bfloat16)
    return (activations, input_grads, balance, gradients[0], gradients[1], gradients[2], gradients[3], gradients[4], gradients[5], gradients[6], gradients[7], gradients[8], gradients[9], gradients[10], gradients[11])
```

```python
import jax
import jax.numpy as jnp
from jax import lax
from jax.sharding import PartitionSpec as P

HEADS = 12
HEAD_DIM = 64
SEQ = 128
MICRO = 2


balance_factor = 20.0
epsilon = 1e-06
highest = lax.Precision.HIGHEST


tokens_over = ("expert", "dp")


def swap(block):
    return lax.ppermute(block, "section", [(0, 1), (1, 0)])


def exchange(block):
    return lax.all_to_all(block, tokens_over, split_axis=0, concat_axis=0, tiled=True)


def rms_scale(tensor):
    return lax.rsqrt(jnp.mean(tensor * tensor, axis=-1, keepdims=True) + epsilon)


def product(left, right):
    return jnp.dot(left, right, preferred_element_type=jnp.float32)


def split_heads(tensor):
    return tensor.reshape(-1, SEQ, HEADS, HEAD_DIM)


def dispatch_table(route_col, experts, capacity):
    onehot = (route_col[:, None] == jnp.arange(experts, dtype=jnp.int32)[None, :]).astype(
        jnp.float32
    )
    slot_rank = jnp.sum((jnp.cumsum(onehot, axis=0) - 1.0) * onehot, axis=-1)
    slot_hot = (slot_rank[:, None] == jnp.arange(capacity, dtype=jnp.float32)[None, :]).astype(
        jnp.float32
    )
    placing = (onehot[:, :, None] * slot_hot[:, None, :]).reshape(
        route_col.shape[0], experts * capacity
    )
    return (onehot, placing.astype(jnp.bfloat16))


def attend(queries, key_rows, values):
    scaling = HEAD_DIM ** (-0.5)
    scores = (
        jnp.einsum(
            "sqhd,skhd->shqk",
            split_heads(queries),
            split_heads(key_rows),
            preferred_element_type=jnp.float32,
        )
        * scaling
    )
    log_total = jax.nn.logsumexp(scores, axis=-1, keepdims=True)
    weights = jnp.exp(scores - log_total).astype(jnp.bfloat16)
    attended = jnp.einsum(
        "shqk,skhd->sqhd", weights, split_heads(values), preferred_element_type=jnp.float32
    )
    return (attended.reshape(queries.shape).astype(jnp.bfloat16), log_total)


def attend_back(queries, key_rows, values, log_total, grad_attended):
    scaling = HEAD_DIM ** (-0.5)
    query_heads = split_heads(queries)
    key_heads = split_heads(key_rows)
    value_heads = split_heads(values)
    grad_heads = split_heads(grad_attended)
    scores = (
        jnp.einsum("sqhd,skhd->shqk", query_heads, key_heads, preferred_element_type=jnp.float32)
        * scaling
    )
    weights = jnp.exp(scores - log_total)
    grad_weights = jnp.einsum(
        "sqhd,skhd->shqk", grad_heads, value_heads, preferred_element_type=jnp.float32
    )
    row_delta = jnp.sum(weights * grad_weights, axis=-1, keepdims=True)
    grad_scores = (weights * (grad_weights - row_delta)).astype(jnp.bfloat16)
    grad_queries = (
        jnp.einsum("shqk,skhd->sqhd", grad_scores, key_heads, preferred_element_type=jnp.float32)
        * scaling
    )
    grad_keys = (
        jnp.einsum("shqk,sqhd->skhd", grad_scores, query_heads, preferred_element_type=jnp.float32)
        * scaling
    )
    grad_values = jnp.einsum(
        "shqk,sqhd->skhd",
        weights.astype(jnp.bfloat16),
        grad_heads,
        preferred_element_type=jnp.float32,
    )
    shape_rows = queries.shape
    return (
        grad_queries.reshape(shape_rows).astype(jnp.bfloat16),
        grad_keys.reshape(shape_rows).astype(jnp.bfloat16),
        grad_values.reshape(shape_rows).astype(jnp.bfloat16),
    )


def per_expert_holders(placing, rows, experts, holders):
    feature = rows.shape[1]
    slots = product(placing.T, rows).astype(jnp.bfloat16).reshape(experts, 1, -1, feature)
    return jnp.broadcast_to(slots, (experts, holders, slots.shape[2], feature)).reshape(
        experts * holders, -1, feature
    )


def attention_forward(x, dense):
    inputs = x.astype(jnp.float32)
    first_scale = rms_scale(inputs)
    normed = (inputs * first_scale * dense["attention_gain"]).astype(jnp.bfloat16)
    queries = (product(normed, dense["query_weight"]) + dense["query_bias"]).astype(jnp.bfloat16)
    key_rows = product(normed, dense["key_weight"]).astype(jnp.bfloat16)
    values = (product(normed, dense["value_weight"]) + dense["value_bias"]).astype(jnp.bfloat16)
    attended, log_total = attend(queries, key_rows, values)
    hidden = inputs + product(attended, dense["out_weight"]) + dense["out_bias"]
    second_scale = rms_scale(hidden)
    normed_moe = (hidden * second_scale * dense["mixture_gain"]).astype(jnp.bfloat16)
    router_probs = jax.nn.softmax(product(normed_moe, dense["router_weight"]), axis=-1)
    return dict(
        inputs=inputs,
        first_scale=first_scale,
        normed=normed,
        queries=queries,
        key_rows=key_rows,
        values=values,
        log_total=log_total,
        attended=attended,
        hidden=hidden,
        second_scale=second_scale,
        normed_moe=normed_moe,
        router_probs=router_probs,
    )


def token_backward(grad_result, combined, grad_normed, stored, onehot, share, dense):
    experts = onehot.shape[1]
    grad_gate = jnp.sum(grad_result * combined, axis=-1)
    router_probs = stored["router_probs"]
    grad_probs = onehot * grad_gate[:, None] + balance_factor * experts * share
    grad_logits = router_probs * (
        grad_probs - jnp.sum(router_probs * grad_probs, axis=-1, keepdims=True)
    )
    router_grad = jnp.dot(
        stored["normed_moe"].astype(jnp.float32).T, grad_logits, precision=highest
    )
    grad_normed = grad_normed + jnp.dot(
        grad_logits, dense["router_weight"].astype(jnp.float32).T, precision=highest
    )
    hidden = stored["hidden"]
    second_scale = stored["second_scale"]
    mixture_grad = jnp.sum(grad_normed * hidden * second_scale, axis=0)
    grad_scaled = grad_normed * dense["mixture_gain"]
    grad_hidden = (
        grad_result
        + second_scale * grad_scaled
        - hidden * second_scale**3 * jnp.mean(grad_scaled * hidden, axis=-1, keepdims=True)
    )
    grad_branch = grad_hidden.astype(jnp.bfloat16)
    out_bias_grad = jnp.sum(grad_branch.astype(jnp.float32), axis=0)
    grad_attended = product(grad_branch, dense["out_weight"].T).astype(jnp.bfloat16)
    grad_queries, grad_keys, grad_values = attend_back(
        stored["queries"], stored["key_rows"], stored["values"], stored["log_total"], grad_attended
    )
    query_bias_grad = jnp.sum(grad_queries.astype(jnp.float32), axis=0)
    value_bias_grad = jnp.sum(grad_values.astype(jnp.float32), axis=0)
    grad_first = (
        product(grad_queries, dense["query_weight"].T)
        + product(grad_keys, dense["key_weight"].T)
        + product(grad_values, dense["value_weight"].T)
    )
    inputs = stored["inputs"]
    first_scale = stored["first_scale"]
    attention_grad = jnp.sum(grad_first * inputs * first_scale, axis=0)
    grad_scaled = grad_first * dense["attention_gain"]
    grad_input = (
        grad_hidden
        + first_scale * grad_scaled
        - inputs * first_scale**3 * jnp.mean(grad_scaled * inputs, axis=-1, keepdims=True)
    ).astype(jnp.bfloat16)
    rows = jnp.stack(
        [stored["normed"], grad_queries, grad_keys, grad_values, stored["attended"], grad_branch]
    )
    feature = hidden.shape[1]
    statistics = jnp.concatenate([jnp.sum(onehot, axis=0), jnp.sum(router_probs, axis=0)])
    small = jnp.concatenate(
        [
            jnp.stack(
                [query_bias_grad, value_bias_grad, out_bias_grad, attention_grad, mixture_grad]
            ),
            router_grad.T,
            jnp.pad(statistics, (0, feature - 2 * experts))[None],
        ]
    )
    return grad_input, rows, small


def expert_forward(rows, owned_in, owned_down):
    pre_act = product(rows, owned_in)
    activated = jax.nn.gelu(pre_act).astype(jnp.bfloat16)
    return pre_act, activated, product(activated, owned_down).astype(jnp.bfloat16)


def expert_backward(rows, pre_act, activated, grad_rows, owned_in, owned_down):
    grad_act = product(grad_rows, owned_down.T)
    unused, gelu_back = jax.vjp(jax.nn.gelu, pre_act)
    grad_pre = gelu_back(grad_act)[0].astype(jnp.bfloat16)
    down_grad = product(activated.T, grad_rows)
    in_grad = product(rows.T, grad_pre)
    return product(grad_pre, owned_in.T).astype(jnp.bfloat16), in_grad, down_grad


def in_two(tensor):
    high = lax.reduce_precision(tensor, 8, 7)
    return high.astype(jnp.bfloat16), (tensor - high).astype(jnp.bfloat16)


def sum_over_tokens(big, small):
    devices = lax.axis_size("expert") * lax.axis_size("dp")
    feature = big.shape[1]
    share = big.shape[0] // devices
    low_rows = jnp.concatenate(in_two(small))
    low_rows = jnp.pad(low_rows, ((0, devices - low_rows.shape[0]), (0, 0)))
    parts = jnp.concatenate(
        [big.reshape(devices, share, feature), low_rows[:, None]], axis=1
    )
    arrived = exchange(parts).astype(jnp.float32)
    total = jnp.sum(arrived, axis=0)
    high, low = in_two(total[share:])
    mine = jnp.concatenate([total[:share].astype(jnp.bfloat16), high, low])
    everyone = exchange(jnp.broadcast_to(mine[None], (devices,) + mine.shape))
    summed = everyone[:, :share].reshape(big.shape).astype(jnp.float32)
    pairs = everyone[:, share].astype(jnp.float32) + everyone[:, share + 1].astype(jnp.float32)
    count = small.shape[0]
    return summed, pairs[:count] + pairs[count : 2 * count]


def on_device(
    section_ends,
    routes,
    query_weight,
    key_weight,
    value_weight,
    out_weight,
    query_bias,
    value_bias,
    out_bias,
    attention_gain,
    mixture_gain,
    router_weight,
    expert_in,
    expert_down,
):
    section_id = lax.axis_index("section")
    first = section_id == 0

    def by_layer(own):
        other = swap(own)
        return jnp.where(first, own, other), jnp.where(first, other, own)

    feature = section_ends.shape[2]
    row_count = section_ends.shape[1] // MICRO
    experts = router_weight.shape[2]
    capacity = row_count * 3 // (2 * experts)
    holders = lax.axis_size("dp")
    devices = lax.axis_size("expert") * holders

    def my_micro(blocks):
        blocks = blocks.reshape((MICRO, row_count) + blocks.shape[1:])
        own = lax.dynamic_index_in_dim(blocks, section_id, 0, keepdims=False)
        other = swap(lax.dynamic_index_in_dim(blocks, 1 - section_id, 0, keepdims=False))
        return jnp.where(first, own, other), jnp.where(first, other, own)

    x, cotangent = my_micro(section_ends[0])
    route_cols = my_micro(routes[0, :, 0])
    names = (
        "query_weight",
        "key_weight",
        "value_weight",
        "out_weight",
        "query_bias",
        "value_bias",
        "out_bias",
        "attention_gain",
        "mixture_gain",
        "router_weight",
    )
    arrays = (
        query_weight,
        key_weight,
        value_weight,
        out_weight,
        query_bias,
        value_bias,
        out_bias,
        attention_gain,
        mixture_gain,
        router_weight,
    )
    both = [by_layer(member[0]) for member in arrays]
    dense = [dict(zip(names, (pair[layer] for pair in both))) for layer in range(2)]
    owned_in = by_layer(expert_in[0, 0])
    owned_down = by_layer(expert_down[0, 0])

    tables = [dispatch_table(col, experts, capacity) for col in route_cols]
    onehots = [table[0] for table in tables]
    placings = [table[1] for table in tables]
    gathers = [
        jnp.broadcast_to(
            placing.reshape(row_count, experts, 1, capacity),
            (row_count, experts, holders, capacity),
        ).reshape(row_count, devices * capacity)
        for placing in placings
    ]
    counts = jnp.concatenate([jnp.sum(onehot, axis=0) for onehot in onehots])
    token_total = devices * row_count

    kept0 = attention_forward(x, dense[0])
    gate0 = jnp.sum(kept0["router_probs"] * onehots[0], axis=-1)
    count_row = jnp.pad(counts, (0, feature - 2 * experts)).astype(jnp.bfloat16)
    outgoing = jnp.concatenate(
        [
            per_expert_holders(placings[0], kept0["normed_moe"], experts, holders),
            jnp.broadcast_to(count_row, (devices, 1, feature)),
        ],
        axis=1,
    )
    arrived = exchange(outgoing)
    shares = jnp.sum(arrived[:, capacity, : 2 * experts].astype(jnp.float32), axis=0) / token_total
    shares = (shares[:experts], shares[experts:])
    rows0 = arrived[:, :capacity].reshape(devices * capacity, feature)
    pre0, act0, partial = expert_forward(rows0, owned_in[0], owned_down[0])
    returned = exchange(partial.reshape(devices, capacity, feature)).reshape(-1, feature)
    combined0 = product(gathers[0], returned)
    result0 = (kept0["hidden"] + gate0[:, None] * combined0).astype(jnp.bfloat16)

    kept1 = attention_forward(result0, dense[1])
    gate1 = jnp.sum(kept1["router_probs"] * onehots[1], axis=-1)
    grad1 = cotangent.astype(jnp.float32)
    grad_tokens = (gate1[:, None] * grad1).astype(jnp.bfloat16)
    outgoing = jnp.concatenate(
        [
            per_expert_holders(placings[1], kept1["normed_moe"], experts, holders),
            per_expert_holders(placings[1], grad_tokens, experts, holders),
        ],
        axis=1,
    )
    arrived = exchange(outgoing)
    rows1 = arrived[:, :capacity].reshape(devices * capacity, feature)
    grad_rows1 = arrived[:, capacity:].reshape(devices * capacity, feature)
    pre1, act1, partial = expert_forward(rows1, owned_in[1], owned_down[1])
    grad_partial, in_grad1, down_grad1 = expert_backward(
        rows1, pre1, act1, grad_rows1, owned_in[1], owned_down[1]
    )
    returned = exchange(
        jnp.concatenate(
            [
                partial.reshape(devices, capacity, feature),
                grad_partial.reshape(devices, capacity, feature),
            ],
            axis=1,
        )
    )
    combined1 = product(gathers[1], returned[:, :capacity].reshape(-1, feature))
    grad_normed = product(gathers[1], returned[:, capacity:].reshape(-1, feature))
    result1 = (kept1["hidden"] + gate1[:, None] * combined1).astype(jnp.bfloat16)
    grad_input1, dense_rows1, small1 = token_backward(
        grad1, combined1, grad_normed, kept1, onehots[1], shares[1], dense[1]
    )

    grad0 = grad_input1.astype(jnp.float32)
    grad_tokens = (gate0[:, None] * grad0).astype(jnp.bfloat16)
    arrived = exchange(per_expert_holders(placings[0], grad_tokens, experts, holders))
    grad_rows0 = arrived.reshape(devices * capacity, feature)
    grad_partial, in_grad0, down_grad0 = expert_backward(
        rows0, pre0, act0, grad_rows0, owned_in[0], owned_down[0]
    )
    returned = exchange(grad_partial.reshape(devices, capacity, feature)).reshape(-1, feature)
    grad_normed = product(gathers[0], returned)
    grad_input0, dense_rows0, small0 = token_backward(
        grad0, combined0, grad_normed, kept0, onehots[0], shares[0], dense[0]
    )

    def own_and_other(layer0, layer1):
        own = jnp.where(first, layer0, layer1)
        return own, swap(jnp.where(first, layer1, layer0))

    def in_order(own, other):
        return jnp.where(first, jnp.stack([own, other]), jnp.stack([other, own]))

    small_own, small_other = own_and_other(small0, small1)
    statistics = in_order(small_own[-1], small_other[-1])
    small = jnp.concatenate([small_own[:-1] + small_other[:-1], statistics])
    rows_own, rows_other = own_and_other(dense_rows0, dense_rows1)
    rows = jnp.concatenate([rows_own, rows_other], axis=1)
    big = jnp.concatenate(
        [
            product(rows[0].T, rows[1]),
            product(rows[0].T, rows[2]),
            product(rows[0].T, rows[3]),
            product(rows[4].T, rows[5]),
        ]
    ).astype(jnp.bfloat16)
    big, small = sum_over_tokens(big, small)
    big = big.reshape(4, feature, feature)
    statistics = small[-MICRO:] / token_total
    balances = experts * jnp.sum(
        statistics[:, :experts] * statistics[:, experts : 2 * experts], axis=1
    )

    outputs = in_order(*own_and_other(result0, result1))
    grads_in = in_order(*own_and_other(grad_input0, grad_input1))
    in_own, in_other = own_and_other(in_grad0, in_grad1)
    down_own, down_other = own_and_other(down_grad0, down_grad1)
    return (
        outputs.reshape(1, -1, feature),
        grads_in.reshape(1, -1, feature),
        balances[None],
        big[0][None],
        big[1][None],
        big[2][None],
        big[3][None],
        small[0][None],
        small[1][None],
        small[2][None],
        small[3][None],
        small[4][None],
        small[5 : 5 + experts].T[None],
        (in_own + in_other)[None, None],
        (down_own + down_other)[None, None],
    )


def solution(mesh):
    placed = (
        P("section", ("expert", "dp"), None),
        P("section", ("expert", "dp"), None),
        P("section", None, None),
        P("section", None, None),
        P("section", None, None),
        P("section", None, None),
        P("section", None),
        P("section", None),
        P("section", None),
        P("section", None),
        P("section", None),
        P("section", None, None),
        P("section", "expert", None, "dp"),
        P("section", "expert", "dp", None),
    )
    return jax.shard_map(
        on_device,
        mesh=mesh,
        in_specs=placed,
        out_specs=(
            P("section", ("expert", "dp"), None),
            P("section", ("expert", "dp"), None),
            P("section", None),
            P("section", None, None),
            P("section", None, None),
            P("section", None, None),
            P("section", None, None),
            P("section", None),
            P("section", None),
            P("section", None),
            P("section", None),
            P("section", None),
            P("section", None, None),
            P("section", "expert", None, "dp"),
            P("section", "expert", "dp", None),
        ),
        check_vma=False,
    )
```

```python
import jax
import jax.numpy as jnp
from jax import lax
from jax.sharding import PartitionSpec as P

HEADS = 12
HEAD_DIM = 64
SEQ = 128
MICRO = 2


balance_factor = 20.0
epsilon = 1e-06
highest = lax.Precision.HIGHEST


tokens_over = ("expert", "dp")


def swap(block):
    return lax.ppermute(block, "section", [(0, 1), (1, 0)])


def exchange(block):
    return lax.all_to_all(block, tokens_over, split_axis=0, concat_axis=0, tiled=True)


def rms_scale(tensor):
    return lax.rsqrt(jnp.mean(tensor * tensor, axis=-1, keepdims=True) + epsilon)


def product(left, right):
    return jnp.dot(left, right, preferred_element_type=jnp.float32)


def split_heads(tensor):
    return tensor.reshape(-1, SEQ, HEADS, HEAD_DIM)


def dispatch_table(route_col, experts, capacity):
    onehot = (route_col[:, None] == jnp.arange(experts, dtype=jnp.int32)[None, :]).astype(
        jnp.float32
    )
    slot_rank = jnp.sum((jnp.cumsum(onehot, axis=0) - 1.0) * onehot, axis=-1)
    slot_hot = (slot_rank[:, None] == jnp.arange(capacity, dtype=jnp.float32)[None, :]).astype(
        jnp.float32
    )
    placing = (onehot[:, :, None] * slot_hot[:, None, :]).reshape(
        route_col.shape[0], experts * capacity
    )
    return (onehot, placing.astype(jnp.bfloat16))


def attend(queries, key_rows, values):
    scaling = HEAD_DIM ** (-0.5)
    scores = (
        jnp.einsum(
            "sqhd,skhd->shqk",
            split_heads(queries),
            split_heads(key_rows),
            preferred_element_type=jnp.float32,
        )
        * scaling
    )
    log_total = jax.nn.logsumexp(scores, axis=-1, keepdims=True)
    weights = jnp.exp(scores - log_total).astype(jnp.bfloat16)
    attended = jnp.einsum(
        "shqk,skhd->sqhd", weights, split_heads(values), preferred_element_type=jnp.float32
    )
    return (attended.reshape(queries.shape).astype(jnp.bfloat16), log_total)


def attend_back(queries, key_rows, values, log_total, grad_attended):
    scaling = HEAD_DIM ** (-0.5)
    query_heads = split_heads(queries)
    key_heads = split_heads(key_rows)
    value_heads = split_heads(values)
    grad_heads = split_heads(grad_attended)
    scores = (
        jnp.einsum("sqhd,skhd->shqk", query_heads, key_heads, preferred_element_type=jnp.float32)
        * scaling
    )
    weights = jnp.exp(scores - log_total)
    grad_weights = jnp.einsum(
        "sqhd,skhd->shqk", grad_heads, value_heads, preferred_element_type=jnp.float32
    )
    row_delta = jnp.sum(weights * grad_weights, axis=-1, keepdims=True)
    grad_scores = (weights * (grad_weights - row_delta)).astype(jnp.bfloat16)
    grad_queries = (
        jnp.einsum("shqk,skhd->sqhd", grad_scores, key_heads, preferred_element_type=jnp.float32)
        * scaling
    )
    grad_keys = (
        jnp.einsum("shqk,sqhd->skhd", grad_scores, query_heads, preferred_element_type=jnp.float32)
        * scaling
    )
    grad_values = jnp.einsum(
        "shqk,sqhd->skhd",
        weights.astype(jnp.bfloat16),
        grad_heads,
        preferred_element_type=jnp.float32,
    )
    shape_rows = queries.shape
    return (
        grad_queries.reshape(shape_rows).astype(jnp.bfloat16),
        grad_keys.reshape(shape_rows).astype(jnp.bfloat16),
        grad_values.reshape(shape_rows).astype(jnp.bfloat16),
    )


def to_holders(gathers, rows):
    devices = lax.axis_size("expert") * lax.axis_size("dp")
    slots = product(gathers.T, rows).astype(jnp.bfloat16)
    return slots.reshape(devices, -1, rows.shape[1])


def attention_forward(x, dense):
    inputs = x.astype(jnp.float32)
    first_scale = rms_scale(inputs)
    normed = (inputs * first_scale * dense["attention_gain"]).astype(jnp.bfloat16)
    queries = (product(normed, dense["query_weight"]) + dense["query_bias"]).astype(jnp.bfloat16)
    key_rows = product(normed, dense["key_weight"]).astype(jnp.bfloat16)
    values = (product(normed, dense["value_weight"]) + dense["value_bias"]).astype(jnp.bfloat16)
    attended, log_total = attend(queries, key_rows, values)
    hidden = inputs + product(attended, dense["out_weight"]) + dense["out_bias"]
    second_scale = rms_scale(hidden)
    normed_moe = (hidden * second_scale * dense["mixture_gain"]).astype(jnp.bfloat16)
    router_probs = jax.nn.softmax(product(normed_moe, dense["router_weight"]), axis=-1)
    return dict(
        inputs=inputs,
        first_scale=first_scale,
        normed=normed,
        queries=queries,
        key_rows=key_rows,
        values=values,
        log_total=log_total,
        attended=attended,
        hidden=hidden,
        second_scale=second_scale,
        normed_moe=normed_moe,
        router_probs=router_probs,
    )


def token_backward(grad_result, combined, grad_normed, stored, onehot, share, dense):
    experts = onehot.shape[1]
    grad_gate = jnp.sum(grad_result * combined, axis=-1)
    router_probs = stored["router_probs"]
    grad_probs = onehot * grad_gate[:, None] + balance_factor * experts * share
    grad_logits = router_probs * (
        grad_probs - jnp.sum(router_probs * grad_probs, axis=-1, keepdims=True)
    )
    router_grad = jnp.dot(
        stored["normed_moe"].astype(jnp.float32).T, grad_logits, precision=highest
    )
    grad_normed = grad_normed + jnp.dot(
        grad_logits, dense["router_weight"].astype(jnp.float32).T, precision=highest
    )
    hidden = stored["hidden"]
    second_scale = stored["second_scale"]
    mixture_grad = jnp.sum(grad_normed * hidden * second_scale, axis=0)
    grad_scaled = grad_normed * dense["mixture_gain"]
    grad_hidden = (
        grad_result
        + second_scale * grad_scaled
        - hidden * second_scale**3 * jnp.mean(grad_scaled * hidden, axis=-1, keepdims=True)
    )
    grad_branch = grad_hidden.astype(jnp.bfloat16)
    out_bias_grad = jnp.sum(grad_branch.astype(jnp.float32), axis=0)
    grad_attended = product(grad_branch, dense["out_weight"].T).astype(jnp.bfloat16)
    grad_queries, grad_keys, grad_values = attend_back(
        stored["queries"], stored["key_rows"], stored["values"], stored["log_total"], grad_attended
    )
    query_bias_grad = jnp.sum(grad_queries.astype(jnp.float32), axis=0)
    value_bias_grad = jnp.sum(grad_values.astype(jnp.float32), axis=0)
    grad_first = (
        product(grad_queries, dense["query_weight"].T)
        + product(grad_keys, dense["key_weight"].T)
        + product(grad_values, dense["value_weight"].T)
    )
    inputs = stored["inputs"]
    first_scale = stored["first_scale"]
    attention_grad = jnp.sum(grad_first * inputs * first_scale, axis=0)
    grad_scaled = grad_first * dense["attention_gain"]
    grad_input = (
        grad_hidden
        + first_scale * grad_scaled
        - inputs * first_scale**3 * jnp.mean(grad_scaled * inputs, axis=-1, keepdims=True)
    ).astype(jnp.bfloat16)
    rows = (
        stored["normed"],
        grad_queries,
        grad_keys,
        grad_values,
        stored["attended"],
        grad_branch,
    )
    feature = hidden.shape[1]
    statistics = jnp.concatenate([jnp.sum(onehot, axis=0), jnp.sum(router_probs, axis=0)])
    small = jnp.concatenate(
        [
            jnp.stack(
                [query_bias_grad, value_bias_grad, out_bias_grad, attention_grad, mixture_grad]
            ),
            router_grad.T,
            jnp.pad(statistics, (0, feature - 2 * experts))[None],
        ]
    )
    return grad_input, rows, small


def expert_forward(rows, owned_in, owned_down):
    pre_act = product(rows, owned_in)
    activated = jax.nn.gelu(pre_act).astype(jnp.bfloat16)
    return pre_act, activated, product(activated, owned_down).astype(jnp.bfloat16)


def expert_backward(rows, pre_act, activated, grad_rows, owned_in, owned_down):
    grad_act = product(grad_rows, owned_down.T)
    unused, gelu_back = jax.vjp(jax.nn.gelu, pre_act)
    grad_pre = gelu_back(grad_act)[0].astype(jnp.bfloat16)
    down_grad = product(activated.T, grad_rows)
    in_grad = product(rows.T, grad_pre)
    return product(grad_pre, owned_in.T).astype(jnp.bfloat16), in_grad, down_grad


def in_two(tensor):
    high = lax.reduce_precision(tensor, 8, 7)
    return high.astype(jnp.bfloat16), (tensor - high).astype(jnp.bfloat16)


def dense_gradients(rows, first):
    normed, grad_queries, grad_keys, grad_values, attended, grad_branch = rows

    def pick(left, right):
        return jnp.where(first, left, right)

    own = (
        normed,
        pick(grad_queries, grad_values),
        pick(normed, attended),
        pick(grad_keys, grad_branch),
    )
    other = (
        swap(normed),
        swap(pick(grad_values, grad_queries)),
        swap(pick(attended, normed)),
        swap(pick(grad_branch, grad_keys)),
    )
    return (
        product(own[0].T, own[1]) + product(other[0].T, other[1]),
        product(own[2].T, own[3]) + product(other[2].T, other[3]),
    )


def sum_beside(big, small):
    count = small.shape[0]
    small = jnp.pad(small, ((0, -count % 32), (0, 0)))
    total = lax.psum(jnp.concatenate(big + (small,)), tokens_over)
    feature = small.shape[1]
    return (
        total[:feature].astype(jnp.bfloat16),
        total[feature : 2 * feature].astype(jnp.bfloat16),
        total[2 * feature : 2 * feature + count],
    )


def sum_at_once(big, small):
    devices = lax.axis_size("expert") * lax.axis_size("dp")
    feature = small.shape[1]
    share = 2 * feature // devices
    lanes = 128
    flat = small.reshape(-1)
    per_device = -(-flat.shape[0] // (devices * lanes))
    flat = jnp.pad(flat, (0, devices * per_device * lanes - flat.shape[0]))
    blocks = jnp.pad(
        flat.reshape(devices, per_device, lanes), ((0, 0), (0, 8 - per_device), (0, 0))
    )

    def beside(high, low):
        return jnp.concatenate([high, low, jnp.zeros_like(high)], axis=-2)

    parts = jnp.concatenate(
        [
            jnp.concatenate(big).astype(jnp.bfloat16).reshape(devices, share, feature),
            beside(*in_two(blocks)),
        ],
        axis=2,
    )
    arrived = jnp.sum(exchange(parts).astype(jnp.float32), axis=0)
    sums = beside(*in_two(arrived[:8, feature:] + arrived[8:16, feature:]))
    mine = jnp.concatenate([arrived[:, :feature].astype(jnp.bfloat16), sums], axis=1)
    everyone = exchange(jnp.broadcast_to(mine[None], (devices,) + mine.shape))
    total = everyone[:, :, :feature].reshape(2 * feature, feature)
    pairs = everyone[:, :, feature:].astype(jnp.float32)
    flat = (pairs[:, :per_device] + pairs[:, 8 : 8 + per_device]).reshape(-1)
    return total[:feature], total[feature:], flat[: small.size].reshape(small.shape)


def on_device(
    section_ends,
    routes,
    query_weight,
    key_weight,
    value_weight,
    out_weight,
    query_bias,
    value_bias,
    out_bias,
    attention_gain,
    mixture_gain,
    router_weight,
    expert_in,
    expert_down,
):
    section_id = lax.axis_index("section")
    first = section_id == 0

    def by_layer(own):
        other = swap(own)
        return jnp.where(first, own, other), jnp.where(first, other, own)

    feature = section_ends.shape[2]
    row_count = section_ends.shape[1] // MICRO
    experts = router_weight.shape[2]
    capacity = 16
    holders = lax.axis_size("dp")
    devices = lax.axis_size("expert") * holders

    def my_micro(blocks):
        blocks = blocks.reshape((MICRO, row_count) + blocks.shape[1:])
        own = lax.dynamic_index_in_dim(blocks, section_id, 0, keepdims=False)
        other = swap(lax.dynamic_index_in_dim(blocks, 1 - section_id, 0, keepdims=False))
        return jnp.where(first, own, other), jnp.where(first, other, own)

    x, cotangent = my_micro(section_ends[0])
    route_cols = my_micro(routes[0, :, 0])
    names = (
        "query_weight",
        "key_weight",
        "value_weight",
        "out_weight",
        "query_bias",
        "value_bias",
        "out_bias",
        "attention_gain",
        "mixture_gain",
        "router_weight",
    )
    arrays = (
        query_weight,
        key_weight,
        value_weight,
        out_weight,
        query_bias,
        value_bias,
        out_bias,
        attention_gain,
        mixture_gain,
        router_weight,
    )
    both = [by_layer(member[0]) for member in arrays]
    dense = [dict(zip(names, (pair[layer] for pair in both))) for layer in range(2)]
    owned_in = by_layer(expert_in[0, 0])
    owned_down = by_layer(expert_down[0, 0])

    tables = [dispatch_table(col, experts, capacity) for col in route_cols]
    onehots = [table[0] for table in tables]
    placings = [table[1] for table in tables]
    gathers = [
        jnp.broadcast_to(
            placing.reshape(row_count, experts, 1, capacity),
            (row_count, experts, holders, capacity),
        ).reshape(row_count, devices * capacity)
        for placing in placings
    ]
    counts = jnp.concatenate([jnp.sum(onehot, axis=0) for onehot in onehots])
    token_total = devices * row_count

    kept0 = attention_forward(x, dense[0])
    gate0 = jnp.sum(kept0["router_probs"] * onehots[0], axis=-1)
    count_row = jnp.pad(counts, (0, feature - 2 * experts)).astype(jnp.bfloat16)
    spare = jnp.arange(capacity)[None, :, None] == capacity - 1
    arrived = exchange(
        jnp.where(spare, count_row, to_holders(gathers[0], kept0["normed_moe"]))
    )
    shares = jnp.sum(arrived[:, -1, : 2 * experts].astype(jnp.float32), axis=0) / token_total
    shares = (shares[:experts], shares[experts:])
    rows0 = arrived.reshape(devices * capacity, feature)
    pre0, act0, partial = expert_forward(rows0, owned_in[0], owned_down[0])
    returned = exchange(partial.reshape(devices, capacity, feature)).reshape(-1, feature)
    combined0 = product(gathers[0], returned)
    result0 = (kept0["hidden"] + gate0[:, None] * combined0).astype(jnp.bfloat16)

    kept1 = attention_forward(result0, dense[1])
    gate1 = jnp.sum(kept1["router_probs"] * onehots[1], axis=-1)
    grad1 = cotangent.astype(jnp.float32)
    grad_tokens = (gate1[:, None] * grad1).astype(jnp.bfloat16)
    outgoing = jnp.concatenate(
        [
            to_holders(gathers[1], kept1["normed_moe"]),
            to_holders(gathers[1], grad_tokens),
        ],
        axis=1,
    )
    arrived = exchange(outgoing)
    rows1 = arrived[:, :capacity].reshape(devices * capacity, feature)
    grad_rows1 = arrived[:, capacity:].reshape(devices * capacity, feature)
    pre1, act1, partial = expert_forward(rows1, owned_in[1], owned_down[1])
    grad_partial, in_grad1, down_grad1 = expert_backward(
        rows1, pre1, act1, grad_rows1, owned_in[1], owned_down[1]
    )
    returned = exchange(
        jnp.concatenate(
            [
                partial.reshape(devices, capacity, feature),
                grad_partial.reshape(devices, capacity, feature),
            ],
            axis=1,
        )
    )
    combined1 = product(gathers[1], returned[:, :capacity].reshape(-1, feature))
    grad_normed = product(gathers[1], returned[:, capacity:].reshape(-1, feature))
    result1 = (kept1["hidden"] + gate1[:, None] * combined1).astype(jnp.bfloat16)
    grad_input1, dense_rows1, small1 = token_backward(
        grad1, combined1, grad_normed, kept1, onehots[1], shares[1], dense[1]
    )

    sums1 = sum_beside(dense_gradients(dense_rows1, first), small1)

    grad0 = grad_input1.astype(jnp.float32)
    grad_tokens = (gate0[:, None] * grad0).astype(jnp.bfloat16)
    arrived = exchange(to_holders(gathers[0], grad_tokens))
    grad_rows0 = arrived.reshape(devices * capacity, feature)
    grad_partial, in_grad0, down_grad0 = expert_backward(
        rows0, pre0, act0, grad_rows0, owned_in[0], owned_down[0]
    )
    returned = exchange(grad_partial.reshape(devices, capacity, feature)).reshape(-1, feature)
    grad_normed = product(gathers[0], returned)
    grad_input0, dense_rows0, small0 = token_backward(
        grad0, combined0, grad_normed, kept0, onehots[0], shares[0], dense[0]
    )

    def own_and_other(layer0, layer1):
        own = jnp.where(first, layer0, layer1)
        return own, swap(jnp.where(first, layer1, layer0))

    def in_order(own, other):
        return jnp.where(first, jnp.stack([own, other]), jnp.stack([other, own]))

    sums0 = sum_at_once(dense_gradients(dense_rows0, first), small0)
    own, other = [], []
    for layer0, layer1 in zip(sums0, sums1):
        pair = own_and_other(layer0, layer1)
        own.append(pair[0])
        other.append(pair[1])
    dense_sums = [
        jnp.where(first, mine, theirs).astype(jnp.float32)
        for mine, theirs in ((own[0], other[0]), (own[1], other[1]), (other[0], own[0]), (other[1], own[1]))
    ]
    small = own[2] + other[2]
    statistics = in_order(own[2][-1], other[2][-1]) / token_total
    balances = experts * jnp.sum(
        statistics[:, :experts] * statistics[:, experts : 2 * experts], axis=1
    )

    outputs = in_order(*own_and_other(result0, result1))
    grads_in = in_order(*own_and_other(grad_input0, grad_input1))
    in_own, in_other = own_and_other(in_grad0, in_grad1)
    down_own, down_other = own_and_other(down_grad0, down_grad1)
    return (
        outputs.reshape(1, -1, feature),
        grads_in.reshape(1, -1, feature),
        balances[None],
        dense_sums[0][None],
        dense_sums[1][None],
        dense_sums[2][None],
        dense_sums[3][None],
        small[0][None],
        small[1][None],
        small[2][None],
        small[3][None],
        small[4][None],
        small[5 : 5 + experts].T[None],
        (in_own + in_other)[None, None],
        (down_own + down_other)[None, None],
    )


def solution(mesh):
    placed = (
        P("section", ("expert", "dp"), None),
        P("section", ("expert", "dp"), None),
        P("section", None, None),
        P("section", None, None),
        P("section", None, None),
        P("section", None, None),
        P("section", None),
        P("section", None),
        P("section", None),
        P("section", None),
        P("section", None),
        P("section", None, None),
        P("section", "expert", None, "dp"),
        P("section", "expert", "dp", None),
    )
    return jax.shard_map(
        on_device,
        mesh=mesh,
        in_specs=placed,
        out_specs=(
            P("section", ("expert", "dp"), None),
            P("section", ("expert", "dp"), None),
            P("section", None),
            P("section", None, None),
            P("section", None, None),
            P("section", None, None),
            P("section", None, None),
            P("section", None),
            P("section", None),
            P("section", None),
            P("section", None),
            P("section", None),
            P("section", None, None),
            P("section", "expert", None, "dp"),
            P("section", "expert", "dp", None),
        ),
        check_vma=False,
    )
```

```python
import functools

import jax
import jax.numpy as jnp
from jax import lax
from jax.experimental import pallas as pl
from jax.experimental.pallas import tpu as pltpu
from jax.sharding import PartitionSpec as P

HEADS = 12
HEAD_DIM = 64
SEQ = 128
MICRO = 2
SLOTS = 16
TAKEN = 12
BLOCK = 2 * TAKEN


balance_factor = 20.0
epsilon = 1e-06
highest = lax.Precision.HIGHEST


tokens_over = ("expert", "dp")


def swap(block):
    return lax.ppermute(block, "section", [(0, 1), (1, 0)])


def exchange(block):
    return lax.all_to_all(block, tokens_over, split_axis=0, concat_axis=0, tiled=True)


def rms_scale(tensor):
    return lax.rsqrt(jnp.mean(tensor * tensor, axis=-1, keepdims=True) + epsilon)


def product(left, right):
    return jnp.dot(left, right, preferred_element_type=jnp.float32)


def _nt(left, right):
    return lax.dot_general(
        left, right, (((1,), (1,)), ((), ())), preferred_element_type=jnp.float32
    )


def _tn(left, right):
    return lax.dot_general(
        left, right, (((0,), (0,)), ((), ())), preferred_element_type=jnp.float32
    )


def _split(tensor):
    high = tensor.astype(jnp.bfloat16)
    return high, (tensor - high.astype(jnp.float32)).astype(jnp.bfloat16)


def _fetch(pick_ref, sources, held, sems):
    own, other = sources
    for choice, group in ((0, own), (1, other)):

        @pl.when(pick_ref[0] == choice)
        def _():
            for i, ref in enumerate(group):
                pltpu.make_async_copy(ref, held.at[i], sems.at[i]).start()


def _arrive(sources, held, sems, i):
    pltpu.make_async_copy(sources[0][i], held.at[i], sems.at[i]).wait()


def _head_masks(rows):
    lane = lax.broadcasted_iota(jnp.int32, (rows, 2 * HEAD_DIM), 1)
    even = (lane < HEAD_DIM).astype(jnp.float32).astype(jnp.bfloat16)
    return lane < HEAD_DIM, (even, 1.0 - even)


def forward_kernel(later, *refs):
    refs = list(refs)
    pick_ref = refs.pop(0)
    if later:
        hidden_in, gate_in, gather_in, returned_in, cotangent = refs[:5]
        refs = refs[5:]
    else:
        x_ref, count_ref = refs[:2]
        refs = refs[2:]
    onehot, scatter, vectors, router, *refs = refs
    own, other = refs[:4], refs[4:8]
    refs = refs[8:]
    if later:
        combined_out, result_out = refs[:2]
        refs = refs[2:]
    (
        normed_out,
        queries_out,
        keys_out,
        values_out,
        attended_out,
        hidden_out,
        moe_out,
        probs_out,
        gate_out,
        outgoing,
        held,
        sems,
    ) = refs
    weights = (own, other)
    _fetch(pick_ref, weights, held, sems)
    if later:
        combined = product(gather_in[...], returned_in[...])
        combined_out[...] = combined
        low = (hidden_in[...] + gate_in[...] * combined).astype(jnp.bfloat16)
        result_out[...] = low
        inputs = low.astype(jnp.float32)
    else:
        inputs = x_ref[...].astype(jnp.float32)
    rows = inputs.shape[0]
    normed = (inputs * rms_scale(inputs) * vectors[3:4, :]).astype(jnp.bfloat16)
    normed_out[...] = normed
    _arrive(weights, held, sems, 0)
    queries_out[...] = (product(normed, held[0]) + vectors[0:1, :]).astype(jnp.bfloat16)
    _arrive(weights, held, sems, 1)
    keys_out[...] = product(normed, held[1]).astype(jnp.bfloat16)
    _arrive(weights, held, sems, 2)
    values_out[...] = (product(normed, held[2]) + vectors[1:2, :]).astype(jnp.bfloat16)
    first_half, masks = _head_masks(rows)
    scaling = HEAD_DIM ** (-0.5)
    for pair in range(HEADS // 2):
        lanes = slice(2 * HEAD_DIM * pair, 2 * HEAD_DIM * (pair + 1))
        query, key, value = queries_out[:, lanes], keys_out[:, lanes], values_out[:, lanes]
        parts = []
        for mask in masks:
            scores = _nt(query * mask, key) * scaling
            shifted = jnp.exp(scores - jnp.max(scores, axis=-1, keepdims=True))
            weight = shifted / jnp.sum(shifted, axis=-1, keepdims=True)
            parts.append(product(weight.astype(jnp.bfloat16), value))
        attended_out[:, lanes] = jnp.where(first_half, parts[0], parts[1]).astype(jnp.bfloat16)
    _arrive(weights, held, sems, 3)
    hidden = inputs + product(attended_out[...], held[3]) + vectors[2:3, :]
    hidden_out[...] = hidden
    moe = (hidden * rms_scale(hidden) * vectors[4:5, :]).astype(jnp.bfloat16)
    moe_out[...] = moe
    logits = product(moe, router[...])
    shifted = jnp.exp(logits - jnp.max(logits, axis=-1, keepdims=True))
    probs = shifted / jnp.sum(shifted, axis=-1, keepdims=True)
    probs_out[...] = probs
    gate = jnp.sum(probs * onehot[...], axis=-1, keepdims=True)
    gate_out[...] = gate
    if later:
        grad_tokens = (gate * cotangent[...].astype(jnp.float32)).astype(jnp.bfloat16)
        outgoing[...] = product(
            scatter[...], jnp.concatenate([moe, grad_tokens], axis=0)
        ).astype(jnp.bfloat16)
    else:
        slots = product(scatter[...], moe)
        row = lax.broadcasted_iota(jnp.int32, slots.shape, 0)
        outgoing[...] = jnp.where(row % SLOTS == SLOTS - 1, count_ref[...], slots).astype(
            jnp.bfloat16
        )


def backward_kernel(later, *refs):
    refs = list(refs)
    pick_ref = refs.pop(0)
    gather_in, returned_in, grad_in, *refs = refs
    if later:
        next_gate, next_scatter, *refs = refs
    else:
        combined_in = refs.pop(0)
    (
        inputs_in,
        normed_in,
        queries_in,
        keys_in,
        values_in,
        attended_in,
        hidden_in,
        moe_in,
        probs_in,
        gate_in,
        onehot_in,
        share_in,
        vectors,
        router,
        *refs,
    ) = refs
    weights = (refs[:4], refs[4:8])
    refs = refs[8:]
    if later:
        result_out = refs.pop(0)
    (
        dx_out,
        dq_out,
        dk_out,
        dv_out,
        da_out,
        small_out,
        *refs,
    ) = refs
    if later:
        next_outgoing = refs.pop(0)
    held, sems = refs
    _fetch(pick_ref, weights, held, sems)
    rows = grad_in.shape[0]
    feature = grad_in.shape[1]
    grad_result = grad_in[...].astype(jnp.float32)
    hidden = hidden_in[...]
    back = product(gather_in[...], returned_in[...])
    if later:
        combined, grad_normed = back[:rows], back[rows:]
        result_out[...] = (hidden + gate_in[...] * combined).astype(jnp.bfloat16)
    else:
        combined, grad_normed = combined_in[...], back
    probs = probs_in[...]
    onehot = onehot_in[...]
    experts = onehot.shape[1]
    grad_gate = jnp.sum(grad_result * combined, axis=-1, keepdims=True)
    grad_probs = onehot * grad_gate + balance_factor * experts * share_in[...]
    grad_logits = probs * (grad_probs - jnp.sum(probs * grad_probs, axis=-1, keepdims=True))
    high, low = _split(grad_logits)
    small_out[8 : 8 + experts, :] = _tn(high, moe_in[...]) + _tn(low, moe_in[...])
    grad_normed = grad_normed + _nt(high, router[...]) + _nt(low, router[...])
    scale = rms_scale(hidden)
    mixture_grad = jnp.sum(grad_normed * hidden * scale, axis=0, keepdims=True)
    grad_scaled = grad_normed * vectors[4:5, :]
    grad_hidden = (
        grad_result
        + scale * grad_scaled
        - hidden * (scale * scale * scale) * jnp.mean(grad_scaled * hidden, axis=-1, keepdims=True)
    )
    branch = grad_hidden.astype(jnp.bfloat16)
    da_out[...] = branch
    out_bias_grad = jnp.sum(branch.astype(jnp.float32), axis=0, keepdims=True)
    _arrive(weights, held, sems, 3)
    grad_attended = _nt(branch, held[3]).astype(jnp.bfloat16)
    first_half, masks = _head_masks(rows)
    scaling = HEAD_DIM ** (-0.5)
    for pair in range(HEADS // 2):
        lanes = slice(2 * HEAD_DIM * pair, 2 * HEAD_DIM * (pair + 1))
        query, key, value = queries_in[:, lanes], keys_in[:, lanes], values_in[:, lanes]
        grad = grad_attended[:, lanes]
        parts = []
        for mask in masks:
            scores = _nt(query * mask, key) * scaling
            shifted = jnp.exp(scores - jnp.max(scores, axis=-1, keepdims=True))
            weight = shifted / jnp.sum(shifted, axis=-1, keepdims=True)
            grad_weight = _nt(grad * mask, value)
            delta = jnp.sum(weight * grad_weight, axis=-1, keepdims=True)
            grad_score = (weight * (grad_weight - delta)).astype(jnp.bfloat16)
            parts.append(
                (
                    product(grad_score, key) * scaling,
                    _tn(grad_score, query) * scaling,
                    _tn(weight.astype(jnp.bfloat16), grad),
                )
            )
        for out, left, right in zip((dq_out, dk_out, dv_out), *parts):
            out[:, lanes] = jnp.where(first_half, left, right).astype(jnp.bfloat16)
    _arrive(weights, held, sems, 0)
    _arrive(weights, held, sems, 1)
    _arrive(weights, held, sems, 2)
    grad_first = _nt(dq_out[...], held[0]) + _nt(dk_out[...], held[1]) + _nt(dv_out[...], held[2])
    inputs = inputs_in[...].astype(jnp.float32)
    scale = rms_scale(inputs)
    attention_grad = jnp.sum(grad_first * inputs * scale, axis=0, keepdims=True)
    grad_scaled = grad_first * vectors[3:4, :]
    dx_out[...] = (
        grad_hidden
        + scale * grad_scaled
        - inputs * (scale * scale * scale) * jnp.mean(grad_scaled * inputs, axis=-1, keepdims=True)
    ).astype(jnp.bfloat16)
    small_out[0:1, :] = jnp.sum(dq_out[...].astype(jnp.float32), axis=0, keepdims=True)
    small_out[1:2, :] = jnp.sum(dv_out[...].astype(jnp.float32), axis=0, keepdims=True)
    small_out[2:3, :] = out_bias_grad
    small_out[3:4, :] = attention_grad
    small_out[4:5, :] = mixture_grad
    small_out[5:8, :] = jnp.zeros((3, feature), jnp.float32)
    small_out[5:6, :experts] = jnp.sum(onehot, axis=0, keepdims=True)
    small_out[6:7, :experts] = jnp.sum(probs, axis=0, keepdims=True)
    if later:
        grad_tokens = (next_gate[...] * dx_out[...].astype(jnp.float32)).astype(jnp.bfloat16)
        next_outgoing[...] = product(next_scatter[...], grad_tokens).astype(jnp.bfloat16)


def call(kernel, pick, arrays, weights, outs):
    def whole(shape):
        return pl.BlockSpec(shape, lambda i: (0,) * len(shape), pipeline_mode=pl.Buffered(1))

    anywhere = pl.BlockSpec(memory_space=pl.ANY)
    own, other = weights
    return pl.pallas_call(
        kernel,
        out_shape=[jax.ShapeDtypeStruct(shape, dtype) for shape, dtype in outs],
        grid=(1,),
        in_specs=[pl.BlockSpec(memory_space=pltpu.SMEM)]
        + [whole(array.shape) for array in arrays]
        + [anywhere] * (len(own) + len(other)),
        out_specs=[whole(shape) for shape, dtype in outs],
        scratch_shapes=[
            pltpu.VMEM((len(own),) + own[0].shape, own[0].dtype),
            pltpu.SemaphoreType.DMA((len(own),)),
        ],
        compiler_params=pltpu.CompilerParams(vmem_limit_bytes=58 * 1024 * 1024),
    )(pick, *arrays, *own, *other)


def experts_kernel(
    pick_ref, mixed, order, own_in, own_down, other_in, other_down,
    outgoing, rows_out, grads_out, act_out, grad_pre_out, held, sems,
):
    weights = ((own_in, own_down), (other_in, other_down))
    _fetch(pick_ref, weights, held, sems)
    group = order.shape[0]
    half = group // 2
    groups = mixed.shape[0] // group
    for i in range(groups):
        apart = product(order[...], mixed[group * i : group * (i + 1), :]).astype(jnp.bfloat16)
        rows_out[half * i : half * (i + 1), :] = apart[:half]
        grads_out[half * i : half * (i + 1), :] = apart[half:]
    _arrive(weights, held, sems, 0)
    pre = product(rows_out[...], held[0])
    cube = 0.044715 * pre * pre * pre
    root = 0.7978845608028654
    bend = jnp.tanh(root * (pre + cube))
    act_out[...] = (0.5 * pre * (1.0 + bend)).astype(jnp.bfloat16)
    slope = 0.5 * (1.0 + bend) + (0.5 * root) * pre * (1.0 - bend * bend) * (
        1.0 + 3 * 0.044715 * pre * pre
    )
    _arrive(weights, held, sems, 1)
    partial = product(act_out[...], held[1]).astype(jnp.bfloat16)
    grad_pre_out[...] = (slope * _nt(grads_out[...], held[1])).astype(jnp.bfloat16)
    grad_partial = _nt(grad_pre_out[...], held[0]).astype(jnp.bfloat16)
    for i in range(groups):
        part = slice(half * i, half * (i + 1))
        apart = jnp.concatenate([partial[part], grad_partial[part]], axis=0)
        outgoing[group * i : group * (i + 1), :] = _tn(order[...], apart).astype(jnp.bfloat16)


def expert_forward(rows, owned_in, owned_down):
    pre_act = product(rows, owned_in)
    activated = jax.nn.gelu(pre_act).astype(jnp.bfloat16)
    return pre_act, activated, product(activated, owned_down).astype(jnp.bfloat16)


def expert_backward(rows, pre_act, activated, grad_rows, owned_in, owned_down):
    grad_act = product(grad_rows, owned_down.T)
    unused, gelu_back = jax.vjp(jax.nn.gelu, pre_act)
    grad_pre = gelu_back(grad_act)[0].astype(jnp.bfloat16)
    down_grad = product(activated.T, grad_rows)
    in_grad = product(rows.T, grad_pre)
    return product(grad_pre, owned_in.T).astype(jnp.bfloat16), in_grad, down_grad


def in_two(tensor):
    high = lax.reduce_precision(tensor, 8, 7)
    return high.astype(jnp.bfloat16), (tensor - high).astype(jnp.bfloat16)


def dense_gradients(rows, first):
    normed, grad_queries, grad_keys, grad_values, attended, grad_branch = rows

    def pick(left, right):
        return jnp.where(first, left, right)

    own = (
        normed,
        pick(grad_queries, grad_values),
        pick(normed, attended),
        pick(grad_keys, grad_branch),
    )
    other = (
        swap(normed),
        swap(pick(grad_values, grad_queries)),
        swap(pick(attended, normed)),
        swap(pick(grad_branch, grad_keys)),
    )
    return (
        product(own[0].T, own[1]) + product(other[0].T, other[1]),
        product(own[2].T, own[3]) + product(other[2].T, other[3]),
    )


def beside(high, low):
    return jnp.concatenate([high, low, jnp.zeros_like(high)], axis=-2)


def parts_to_sum(big, small):
    devices = lax.axis_size("expert") * lax.axis_size("dp")
    feature = small.shape[1]
    share = 2 * feature // devices
    lanes = 128
    flat = small.reshape(-1)
    per_device = -(-flat.shape[0] // (devices * lanes))
    flat = jnp.pad(flat, (0, devices * per_device * lanes - flat.shape[0]))
    blocks = jnp.pad(
        flat.reshape(devices, per_device, lanes), ((0, 0), (0, 8 - per_device), (0, 0))
    )

    return jnp.concatenate(
        [
            jnp.concatenate(big).astype(jnp.bfloat16).reshape(devices, share, feature),
            beside(*in_two(blocks)),
        ],
        axis=2,
    )


def add_up(arrived):
    devices = arrived.shape[0]
    feature = arrived.shape[2] - 128
    arrived = jnp.sum(arrived.astype(jnp.float32), axis=0)
    sums = beside(*in_two(arrived[:8, feature:] + arrived[8:16, feature:]))
    mine = jnp.concatenate([arrived[:, :feature].astype(jnp.bfloat16), sums], axis=1)
    return jnp.broadcast_to(mine[None], (devices,) + mine.shape)


def sums_of(everyone, count):
    feature = everyone.shape[2] - 128
    per_device = -(-count * feature // (everyone.shape[0] * 128))
    total = everyone[:, :, :feature].reshape(2 * feature, feature)
    pairs = everyone[:, :, feature:].astype(jnp.float32)
    flat = (pairs[:, :per_device] + pairs[:, 8 : 8 + per_device]).reshape(-1)
    return total[:feature], total[feature:], flat[: count * feature].reshape(count, feature)


def on_device(
    section_ends,
    routes,
    query_weight,
    key_weight,
    value_weight,
    out_weight,
    query_bias,
    value_bias,
    out_bias,
    attention_gain,
    mixture_gain,
    router_weight,
    expert_in,
    expert_down,
):
    section_id = lax.axis_index("section")
    first = section_id == 0

    def by_layer(own):
        other = swap(own)
        return jnp.where(first, own, other), jnp.where(first, other, own)

    feature = section_ends.shape[2]
    row_count = section_ends.shape[1] // MICRO
    experts = router_weight.shape[2]
    holders = lax.axis_size("dp")
    devices = lax.axis_size("expert") * holders

    def my_micro(blocks):
        blocks = blocks.reshape((MICRO, row_count) + blocks.shape[1:])
        own = lax.dynamic_index_in_dim(blocks, section_id, 0, keepdims=False)
        other = swap(lax.dynamic_index_in_dim(blocks, 1 - section_id, 0, keepdims=False))
        return jnp.where(first, own, other), jnp.where(first, other, own)

    x, cotangent = my_micro(section_ends[0])
    route_cols = my_micro(routes[0, :, 0])
    own_weights = (query_weight[0], key_weight[0], value_weight[0], out_weight[0])
    weights = (own_weights, tuple(swap(member) for member in own_weights))
    picks = (section_id.astype(jnp.int32)[None], (1 - section_id).astype(jnp.int32)[None])
    vectors = by_layer(
        jnp.concatenate(
            [
                query_bias,
                value_bias,
                out_bias,
                attention_gain,
                mixture_gain,
                jnp.zeros((3, feature), jnp.float32),
            ]
        )
    )
    routers = by_layer(router_weight[0])
    owned_in = by_layer(expert_in[0, 0])
    owned_down = by_layer(expert_down[0, 0])
    own_experts = (expert_in[0, 0], expert_down[0, 0])
    experts_of_both = (own_experts, tuple(swap(member) for member in own_experts))

    onehots, codes = [], []
    position = jnp.arange(row_count)
    for col in route_cols:
        same = col[:, None] == col[None, :]
        rank = jnp.sum(same & (position[None, :] < position[:, None]), axis=1)
        codes.append(col * SLOTS + rank)
        onehots.append((col[:, None] == jnp.arange(experts)[None, :]).astype(jnp.float32))
    row = jnp.arange(devices * SLOTS)
    places0 = row // (holders * SLOTS) * SLOTS + row % SLOTS
    tokens0 = codes[0]
    row = jnp.arange(devices * BLOCK)
    apart = experts * SLOTS
    places1 = row // (holders * BLOCK) * SLOTS + row % TAKEN + row % BLOCK // TAKEN * apart
    group = jnp.arange(16 * BLOCK)
    half = 16 * TAKEN
    source = group % half // TAKEN * BLOCK + group % TAKEN + group // half * TAKEN
    order = (source[:, None] == group[None, :]).astype(jnp.bfloat16)
    tokens1 = jnp.concatenate([codes[1], codes[1] + apart])
    scatters = [
        (places[:, None] == tokens[None, :]).astype(jnp.bfloat16)
        for places, tokens in ((places0, tokens0), (places1, tokens1))
    ]
    gathers = [
        (tokens[:, None] == places[None, :]).astype(jnp.bfloat16)
        for places, tokens in ((places0, tokens0), (places1, tokens1))
    ]
    counts = jnp.concatenate([jnp.sum(onehot, axis=0) for onehot in onehots])
    token_total = devices * row_count
    count_row = jnp.pad(counts, (0, feature - 2 * experts))[None]

    low, full = jnp.bfloat16, jnp.float32
    block = (row_count, feature)
    kept = [
        (block, low),
        (block, low),
        (block, low),
        (block, low),
        (block, low),
        (block, full),
        (block, low),
        ((row_count, experts), full),
        ((row_count, 1), full),
    ]

    *kept0, outgoing = call(
        functools.partial(forward_kernel, False),
        picks[0],
        [x, count_row, onehots[0], scatters[0], vectors[0], routers[0]],
        weights,
        kept + [((devices * SLOTS, feature), low)],
    )
    arrived = exchange(outgoing.reshape(devices, SLOTS, feature))
    shares = jnp.sum(arrived[:, -1, : 2 * experts].astype(jnp.float32), axis=0) / token_total
    shares = (shares[None, :experts], shares[None, experts:])
    rows0 = arrived.reshape(devices * SLOTS, feature)
    pre0, act0, partial = expert_forward(rows0, owned_in[0], owned_down[0])
    returned = exchange(partial.reshape(devices, SLOTS, feature)).reshape(-1, feature)

    combined0, result0, *kept1, outgoing = call(
        functools.partial(forward_kernel, True),
        picks[1],
        [
            kept0[5],
            kept0[8],
            gathers[0],
            returned,
            cotangent,
            onehots[1],
            scatters[1],
            vectors[1],
            routers[1],
        ],
        weights,
        [(block, full), (block, low)] + kept + [((devices * BLOCK, feature), low)],
    )
    arrived = exchange(outgoing.reshape(devices, BLOCK, feature)).reshape(-1, feature)
    outgoing, rows1, grad_rows1, act1, grad_pre1 = call(
        experts_kernel,
        picks[1],
        [arrived, order],
        experts_of_both,
        [((devices * BLOCK, feature), low)] + [((devices * TAKEN, feature), low)] * 4,
    )
    in_grad1 = product(rows1.T, grad_pre1)
    down_grad1 = product(act1.T, grad_rows1)
    returned = exchange(outgoing.reshape(devices, BLOCK, feature)).reshape(-1, feature)
    gradients = [
        (block, low),
        (block, low),
        (block, low),
        (block, low),
        (block, low),
        ((8 + experts, feature), full),
    ]
    result1, grad_input1, *grads1, small1, outgoing = call(
        functools.partial(backward_kernel, True),
        picks[1],
        [
            gathers[1],
            returned,
            cotangent,
            kept0[8],
            scatters[0],
            result0,
            *kept1,
            onehots[1],
            shares[1],
            vectors[1],
            routers[1],
        ],
        weights,
        [(block, low)] + gradients + [((devices * SLOTS, feature), low)],
    )
    dense_rows1 = (kept1[0], *grads1[:3], kept1[4], grads1[3])
    parts1 = parts_to_sum(dense_gradients(dense_rows1, first), small1)

    arrived = exchange(outgoing.reshape(devices, SLOTS, feature))
    arrived, parts1 = lax.optimization_barrier((arrived, parts1))
    shares1 = add_up(exchange(parts1))
    grad_rows0 = arrived.reshape(devices * SLOTS, feature)
    grad_partial, in_grad0, down_grad0 = expert_backward(
        rows0, pre0, act0, grad_rows0, owned_in[0], owned_down[0]
    )
    returned = exchange(grad_partial.reshape(devices, SLOTS, feature)).reshape(-1, feature)
    returned, shares1 = lax.optimization_barrier((returned, shares1))
    everyone1 = exchange(shares1)
    grad_input0, *grads0, small0 = call(
        functools.partial(backward_kernel, False),
        picks[0],
        [
            gathers[0],
            returned,
            grad_input1,
            combined0,
            x,
            *kept0,
            onehots[0],
            shares[0],
            vectors[0],
            routers[0],
        ],
        weights,
        gradients,
    )
    dense_rows0 = (kept0[0], *grads0[:3], kept0[4], grads0[3])

    def own_and_other(layer0, layer1):
        own = jnp.where(first, layer0, layer1)
        return own, swap(jnp.where(first, layer1, layer0))

    def in_order(own, other):
        return jnp.where(first, jnp.stack([own, other]), jnp.stack([other, own]))

    parts0 = parts_to_sum(dense_gradients(dense_rows0, first), small0)
    parts0, everyone1 = lax.optimization_barrier((parts0, everyone1))
    count = small0.shape[0]
    sums1 = sums_of(everyone1, count)
    sums0 = sums_of(exchange(add_up(exchange(parts0))), count)
    own, other = [], []
    for layer0, layer1 in zip(sums0, sums1):
        pair = own_and_other(layer0, layer1)
        own.append(pair[0])
        other.append(pair[1])
    dense_sums = [
        jnp.where(first, mine, theirs).astype(jnp.float32)
        for mine, theirs in (
            (own[0], other[0]),
            (own[1], other[1]),
            (other[0], own[0]),
            (other[1], own[1]),
        )
    ]
    small = own[2] + other[2]
    statistics = in_order(own[2][5:7, :experts], other[2][5:7, :experts]) / token_total
    balances = experts * jnp.sum(statistics[:, 0] * statistics[:, 1], axis=1)

    outputs = in_order(*own_and_other(result0, result1))
    grads_in = in_order(*own_and_other(grad_input0, grad_input1))
    in_own, in_other = own_and_other(in_grad0, in_grad1)
    down_own, down_other = own_and_other(down_grad0, down_grad1)
    return (
        outputs.reshape(1, -1, feature),
        grads_in.reshape(1, -1, feature),
        balances[None],
        dense_sums[0][None],
        dense_sums[1][None],
        dense_sums[2][None],
        dense_sums[3][None],
        small[0][None],
        small[1][None],
        small[2][None],
        small[3][None],
        small[4][None],
        small[8 : 8 + experts].T[None],
        (in_own + in_other)[None, None],
        (down_own + down_other)[None, None],
    )


def solution(mesh):
    placed = (
        P("section", ("expert", "dp"), None),
        P("section", ("expert", "dp"), None),
        P("section", None, None),
        P("section", None, None),
        P("section", None, None),
        P("section", None, None),
        P("section", None),
        P("section", None),
        P("section", None),
        P("section", None),
        P("section", None),
        P("section", None, None),
        P("section", "expert", None, "dp"),
        P("section", "expert", "dp", None),
    )
    return jax.shard_map(
        on_device,
        mesh=mesh,
        in_specs=placed,
        out_specs=(
            P("section", ("expert", "dp"), None),
            P("section", ("expert", "dp"), None),
            P("section", None),
            P("section", None, None),
            P("section", None, None),
            P("section", None, None),
            P("section", None, None),
            P("section", None),
            P("section", None),
            P("section", None),
            P("section", None),
            P("section", None),
            P("section", None, None),
            P("section", "expert", None, "dp"),
            P("section", "expert", "dp", None),
        ),
        check_vma=False,
    )
```

```python
import functools

import jax
import jax.numpy as jnp
from jax import lax
from jax.experimental import pallas as pl
from jax.experimental.pallas import tpu as pltpu
from jax.sharding import PartitionSpec as P

HEADS = 12
HEAD_DIM = 64
SEQ = 128
MICRO = 2
SLOTS = 16
TAKEN = 12
BLOCK = 2 * TAKEN


balance_factor = 20.0
epsilon = 1e-06
highest = lax.Precision.HIGHEST


tokens_over = ("expert", "dp")


def swap(block):
    return lax.ppermute(block, "section", [(0, 1), (1, 0)])


def exchange(block):
    return lax.all_to_all(block, tokens_over, split_axis=0, concat_axis=0, tiled=True)


def exchange_experts(block):
    feature = block.shape[1]
    experts = lax.axis_size("expert")
    parts = block.reshape(experts, -1, feature)
    arrived = lax.all_to_all(parts, "expert", split_axis=0, concat_axis=0, tiled=True)
    return arrived.reshape(-1, feature)


def rms_scale(tensor):
    return lax.rsqrt(jnp.mean(tensor * tensor, axis=-1, keepdims=True) + epsilon)


def product(left, right):
    return jnp.dot(left, right, preferred_element_type=jnp.float32)


def _nt(left, right):
    return lax.dot_general(
        left, right, (((1,), (1,)), ((), ())), preferred_element_type=jnp.float32
    )


def _tn(left, right):
    return lax.dot_general(
        left, right, (((0,), (0,)), ((), ())), preferred_element_type=jnp.float32
    )


def _split(tensor):
    high = tensor.astype(jnp.bfloat16)
    return high, (tensor - high.astype(jnp.float32)).astype(jnp.bfloat16)


def _fetch(pick_ref, sources, held, sems):
    own, other = sources
    for choice, group in ((0, own), (1, other)):

        @pl.when(pick_ref[0] == choice)
        def _():
            for i, ref in enumerate(group):
                pltpu.make_async_copy(ref, held.at[i], sems.at[i]).start()


def _arrive(sources, held, sems, i):
    pltpu.make_async_copy(sources[0][i], held.at[i], sems.at[i]).wait()


def _head_masks(rows):
    lane = lax.broadcasted_iota(jnp.int32, (rows, 2 * HEAD_DIM), 1)
    even = (lane < HEAD_DIM).astype(jnp.float32).astype(jnp.bfloat16)
    return lane < HEAD_DIM, (even, 1.0 - even)


def _chosen(pick_ref, own_ref, other_ref):
    return jnp.where(pick_ref[0] == 0, own_ref[...], other_ref[...])


def _micro_of_layer(later, pick_ref, own_ref, other_ref):
    rows = own_ref.shape[0] // MICRO
    if later:
        return jnp.where(pick_ref[0] == 0, own_ref[rows:, :], other_ref[:rows, :])
    return jnp.where(pick_ref[0] == 0, own_ref[:rows, :], other_ref[rows:, :])


def forward_kernel(later, *refs):
    refs = list(refs)
    pick_ref = refs.pop(0)
    own_ends, other_ends = refs[:2]
    refs = refs[2:]
    if later:
        hidden_in, gate_in, gather_in, returned_in = refs[:4]
        refs = refs[4:]
    else:
        count_ref = refs.pop(0)
    onehot, scatter, *sides = refs[:6]
    vectors = _chosen(pick_ref, *sides[:2])
    router = _chosen(pick_ref, *sides[2:])
    refs = refs[6:]
    own, other = refs[:4], refs[4:8]
    refs = refs[8:]
    if later:
        combined_out, result_out = refs[:2]
        refs = refs[2:]
    (
        normed_out,
        queries_out,
        keys_out,
        values_out,
        attended_out,
        hidden_out,
        moe_out,
        probs_out,
        gate_out,
        outgoing,
        held,
        sems,
    ) = refs
    weights = (own, other)
    _fetch(pick_ref, weights, held, sems)
    if later:
        combined = product(gather_in[...], returned_in[...])
        combined_out[...] = combined
        low = (hidden_in[...] + gate_in[...] * combined).astype(jnp.bfloat16)
        result_out[...] = low
        inputs = low.astype(jnp.float32)
    else:
        inputs = _micro_of_layer(later, pick_ref, own_ends, other_ends).astype(jnp.float32)
    rows = inputs.shape[0]
    normed = (inputs * rms_scale(inputs) * vectors[3:4, :]).astype(jnp.bfloat16)
    normed_out[...] = normed
    _arrive(weights, held, sems, 0)
    queries_out[...] = (product(normed, held[0]) + vectors[0:1, :]).astype(jnp.bfloat16)
    _arrive(weights, held, sems, 1)
    keys_out[...] = product(normed, held[1]).astype(jnp.bfloat16)
    _arrive(weights, held, sems, 2)
    values_out[...] = (product(normed, held[2]) + vectors[1:2, :]).astype(jnp.bfloat16)
    first_half, masks = _head_masks(rows)
    scaling = HEAD_DIM ** (-0.5)
    for pair in range(HEADS // 2):
        lanes = slice(2 * HEAD_DIM * pair, 2 * HEAD_DIM * (pair + 1))
        query, key, value = queries_out[:, lanes], keys_out[:, lanes], values_out[:, lanes]
        parts = []
        for mask in masks:
            scores = _nt(query * mask, key) * scaling
            shifted = jnp.exp(scores - jnp.max(scores, axis=-1, keepdims=True))
            weight = shifted / jnp.sum(shifted, axis=-1, keepdims=True)
            parts.append(product(weight.astype(jnp.bfloat16), value))
        attended_out[:, lanes] = jnp.where(first_half, parts[0], parts[1]).astype(jnp.bfloat16)
    _arrive(weights, held, sems, 3)
    hidden = inputs + product(attended_out[...], held[3]) + vectors[2:3, :]
    hidden_out[...] = hidden
    moe = (hidden * rms_scale(hidden) * vectors[4:5, :]).astype(jnp.bfloat16)
    moe_out[...] = moe
    logits = product(moe, router)
    shifted = jnp.exp(logits - jnp.max(logits, axis=-1, keepdims=True))
    probs = shifted / jnp.sum(shifted, axis=-1, keepdims=True)
    probs_out[...] = probs
    gate = jnp.sum(probs * onehot[...], axis=-1, keepdims=True)
    gate_out[...] = gate
    if later:
        cotangent = _micro_of_layer(later, pick_ref, own_ends, other_ends)
        grad_tokens = (gate * cotangent.astype(jnp.float32)).astype(jnp.bfloat16)
        outgoing[...] = product(
            scatter[...], jnp.concatenate([moe, grad_tokens], axis=0)
        ).astype(jnp.bfloat16)
    else:
        slots = product(scatter[...], moe)
        row = lax.broadcasted_iota(jnp.int32, slots.shape, 0)
        outgoing[...] = jnp.where(row % SLOTS == SLOTS - 1, count_ref[...], slots).astype(
            jnp.bfloat16
        )


def backward_kernel(later, *refs):
    refs = list(refs)
    pick_ref = refs.pop(0)
    own_ends, other_ends, gather_in, returned_in, *refs = refs
    ends = _micro_of_layer(later, pick_ref, own_ends, other_ends)
    if later:
        grad_result = ends.astype(jnp.float32)
        inputs_in = refs.pop(0)
        next_gate, next_scatter, *refs = refs
    else:
        grad_in = refs.pop(0)
        grad_result = grad_in[...].astype(jnp.float32)
        combined_in = refs.pop(0)
        inputs_in = ends
    (
        normed_in,
        queries_in,
        keys_in,
        values_in,
        attended_in,
        hidden_in,
        moe_in,
        probs_in,
        gate_in,
        onehot_in,
        share_in,
        *refs,
    ) = refs
    vectors = _chosen(pick_ref, *refs[:2])
    router = _chosen(pick_ref, *refs[2:4])
    refs = refs[4:]
    weights = (refs[:4], refs[4:8])
    refs = refs[8:]
    if later:
        result_out = refs.pop(0)
    (
        dx_out,
        dq_out,
        dk_out,
        dv_out,
        da_out,
        small_out,
        *refs,
    ) = refs
    if later:
        next_outgoing = refs.pop(0)
    held, sems = refs
    _fetch(pick_ref, weights, held, sems)
    rows, feature = grad_result.shape
    hidden = hidden_in[...]
    back = product(gather_in[...], returned_in[...])
    if later:
        combined, grad_normed = back[:rows], back[rows:]
        result_out[...] = (hidden + gate_in[...] * combined).astype(jnp.bfloat16)
    else:
        combined, grad_normed = combined_in[...], back
    probs = probs_in[...]
    onehot = onehot_in[...]
    experts = onehot.shape[1]
    grad_gate = jnp.sum(grad_result * combined, axis=-1, keepdims=True)
    grad_probs = onehot * grad_gate + balance_factor * experts * share_in[...]
    grad_logits = probs * (grad_probs - jnp.sum(probs * grad_probs, axis=-1, keepdims=True))
    high, low = _split(grad_logits)
    small_out[8 : 8 + experts, :] = _tn(high, moe_in[...]) + _tn(low, moe_in[...])
    grad_normed = grad_normed + _nt(high, router) + _nt(low, router)
    scale = rms_scale(hidden)
    mixture_grad = jnp.sum(grad_normed * hidden * scale, axis=0, keepdims=True)
    grad_scaled = grad_normed * vectors[4:5, :]
    grad_hidden = (
        grad_result
        + scale * grad_scaled
        - hidden * (scale * scale * scale) * jnp.mean(grad_scaled * hidden, axis=-1, keepdims=True)
    )
    branch = grad_hidden.astype(jnp.bfloat16)
    da_out[...] = branch
    out_bias_grad = jnp.sum(branch.astype(jnp.float32), axis=0, keepdims=True)
    _arrive(weights, held, sems, 3)
    grad_attended = _nt(branch, held[3]).astype(jnp.bfloat16)
    first_half, masks = _head_masks(rows)
    scaling = HEAD_DIM ** (-0.5)
    for pair in range(HEADS // 2):
        lanes = slice(2 * HEAD_DIM * pair, 2 * HEAD_DIM * (pair + 1))
        query, key, value = queries_in[:, lanes], keys_in[:, lanes], values_in[:, lanes]
        grad = grad_attended[:, lanes]
        parts = []
        for mask in masks:
            scores = _nt(query * mask, key) * scaling
            shifted = jnp.exp(scores - jnp.max(scores, axis=-1, keepdims=True))
            weight = shifted / jnp.sum(shifted, axis=-1, keepdims=True)
            grad_weight = _nt(grad * mask, value)
            delta = jnp.sum(weight * grad_weight, axis=-1, keepdims=True)
            grad_score = (weight * (grad_weight - delta)).astype(jnp.bfloat16)
            parts.append(
                (
                    product(grad_score, key) * scaling,
                    _tn(grad_score, query) * scaling,
                    _tn(weight.astype(jnp.bfloat16), grad),
                )
            )
        for out, left, right in zip((dq_out, dk_out, dv_out), *parts):
            out[:, lanes] = jnp.where(first_half, left, right).astype(jnp.bfloat16)
    _arrive(weights, held, sems, 0)
    _arrive(weights, held, sems, 1)
    _arrive(weights, held, sems, 2)
    grad_first = _nt(dq_out[...], held[0]) + _nt(dk_out[...], held[1]) + _nt(dv_out[...], held[2])
    inputs = inputs_in[...].astype(jnp.float32)
    scale = rms_scale(inputs)
    attention_grad = jnp.sum(grad_first * inputs * scale, axis=0, keepdims=True)
    grad_scaled = grad_first * vectors[3:4, :]
    dx_out[...] = (
        grad_hidden
        + scale * grad_scaled
        - inputs * (scale * scale * scale) * jnp.mean(grad_scaled * inputs, axis=-1, keepdims=True)
    ).astype(jnp.bfloat16)
    small_out[0:1, :] = jnp.sum(dq_out[...].astype(jnp.float32), axis=0, keepdims=True)
    small_out[1:2, :] = jnp.sum(dv_out[...].astype(jnp.float32), axis=0, keepdims=True)
    small_out[2:3, :] = out_bias_grad
    small_out[3:4, :] = attention_grad
    small_out[4:5, :] = mixture_grad
    small_out[5:8, :] = jnp.zeros((3, feature), jnp.float32)
    small_out[5:6, :experts] = jnp.sum(onehot, axis=0, keepdims=True)
    small_out[6:7, :experts] = jnp.sum(probs, axis=0, keepdims=True)
    if later:
        grad_tokens = (next_gate[...] * dx_out[...].astype(jnp.float32)).astype(jnp.bfloat16)
        next_outgoing[...] = product(next_scatter[...], grad_tokens).astype(jnp.bfloat16)


def call(kernel, pick, arrays, weights, outs, scratch=()):
    def whole(shape):
        return pl.BlockSpec(shape, lambda i: (0,) * len(shape), pipeline_mode=pl.Buffered(1))

    anywhere = pl.BlockSpec(memory_space=pl.ANY)
    own, other = weights
    return pl.pallas_call(
        kernel,
        out_shape=[jax.ShapeDtypeStruct(shape, dtype) for shape, dtype in outs],
        grid=(1,),
        in_specs=[pl.BlockSpec(memory_space=pltpu.SMEM)]
        + [whole(array.shape) for array in arrays]
        + [anywhere] * (len(own) + len(other)),
        out_specs=[whole(shape) for shape, dtype in outs],
        scratch_shapes=[pltpu.VMEM(shape, dtype) for shape, dtype in scratch]
        + [
            pltpu.VMEM((len(own),) + own[0].shape, own[0].dtype),
            pltpu.SemaphoreType.DMA((len(own),) + own[0].shape[:-2]),
        ],
        compiler_params=pltpu.CompilerParams(vmem_limit_bytes=58 * 1024 * 1024),
    )(pick, *arrays, *own, *other)


def gelu_parts(pre):
    root = 0.7978845608028654
    square = pre * pre
    bend = jnp.tanh(root * (pre + 0.044715 * square * pre))
    slope = 0.5 * (1.0 + bend) + (0.5 * root) * pre * (1.0 - bend * bend) * (
        1.0 + 3 * 0.044715 * square
    )
    return 0.5 * pre * (1.0 + bend), slope


def sort_apart(order, mixed, rows_out, grads_out):
    group = order.shape[0]
    half = group // 2
    for i in range(mixed.shape[0] // group):
        apart = product(order[...], mixed[group * i : group * (i + 1), :]).astype(jnp.bfloat16)
        rows_out[half * i : half * (i + 1), :] = apart[:half]
        grads_out[half * i : half * (i + 1), :] = apart[half:]


def slice_kernel(
    pick_ref,
    mixed,
    order,
    own_in,
    own_down,
    other_in,
    other_down,
    rows_out,
    grads_out,
    act_out,
    grad_pre_out,
    held,
    sems,
):
    weights = ((own_in, own_down), (other_in, other_down))
    _fetch(pick_ref, weights, held, sems)
    sort_apart(order, mixed, rows_out, grads_out)
    _arrive(weights, held, sems, 0)
    act, slope = gelu_parts(product(rows_out[...], held[0]))
    act_out[...] = act.astype(jnp.bfloat16)
    _arrive(weights, held, sems, 1)
    grad_pre_out[...] = (slope * _nt(grads_out[...], held[1])).astype(jnp.bfloat16)


def _fetch_wide(pick_ref, weights, held, sems):
    for choice in (0, 1):

        @pl.when(pick_ref[0] == choice)
        def _():
            for part in range(held.shape[1]):
                for i, ref in enumerate(weights[choice]):
                    pltpu.make_async_copy(
                        ref.at[part], held.at[i, part], sems.at[i, part]
                    ).start()


def _arrive_wide(weights, held, sems, part):
    for i, ref in enumerate(weights[0]):
        pltpu.make_async_copy(ref.at[part], held.at[i, part], sems.at[i, part]).wait()


def both_ways_kernel(
    pick_ref, mixed, order, own_in, own_down, other_in, other_down, outgoing, rows, grads, held, sems
):
    weights = ((own_in, own_down), (other_in, other_down))
    _fetch_wide(pick_ref, weights, held, sems)
    sort_apart(order, mixed, rows, grads)
    total = jnp.zeros(rows.shape, jnp.float32)
    grad_total = jnp.zeros(rows.shape, jnp.float32)
    for part in range(held.shape[1]):
        _arrive_wide(weights, held, sems, part)
        act, slope = gelu_parts(product(rows[...], held[0, part]))
        total = total + product(act.astype(jnp.bfloat16), held[1, part])
        grad_pre = (slope * _nt(grads[...], held[1, part])).astype(jnp.bfloat16)
        grad_total = grad_total + _nt(grad_pre, held[0, part])
    apart = jnp.concatenate([total.astype(jnp.bfloat16), grad_total.astype(jnp.bfloat16)], axis=0)
    outgoing[...] = _tn(order[...], apart).astype(jnp.bfloat16)


def back_kernel(
    pick_ref, rows, grads, own_in, own_down, other_in, other_down, outgoing, held, sems
):
    weights = ((own_in, own_down), (other_in, other_down))
    _fetch_wide(pick_ref, weights, held, sems)
    grad_total = jnp.zeros(rows.shape, jnp.float32)
    for part in range(held.shape[1]):
        _arrive_wide(weights, held, sems, part)
        act, slope = gelu_parts(product(rows[...], held[0, part]))
        grad_pre = (slope * _nt(grads[...], held[1, part])).astype(jnp.bfloat16)
        grad_total = grad_total + _nt(grad_pre, held[0, part])
    outgoing[...] = grad_total.astype(jnp.bfloat16)


def expert_forward(rows, owned_in, owned_down):
    pre_act = product(rows, owned_in)
    activated = jax.nn.gelu(pre_act).astype(jnp.bfloat16)
    return pre_act, activated, product(activated, owned_down).astype(jnp.bfloat16)


def expert_gradients(rows, pre_act, activated, grad_rows, owned_down):
    grad_act = product(grad_rows, owned_down.T)
    grad_pre = (gelu_parts(pre_act)[1] * grad_act).astype(jnp.bfloat16)
    return product(rows.T, grad_pre), product(activated.T, grad_rows)


def in_two(tensor):
    high = lax.reduce_precision(tensor, 8, 7)
    return high.astype(jnp.bfloat16), (tensor - high).astype(jnp.bfloat16)


def dense_gradients(rows, first):
    normed, grad_queries, grad_keys, grad_values, attended, grad_branch = rows

    def pick(left, right):
        return jnp.where(first, left, right)

    own = (
        normed,
        pick(grad_queries, grad_values),
        pick(normed, attended),
        pick(grad_keys, grad_branch),
    )
    other = (
        swap(normed),
        swap(pick(grad_values, grad_queries)),
        swap(pick(attended, normed)),
        swap(pick(grad_branch, grad_keys)),
    )
    return (
        product(own[0].T, own[1]) + product(other[0].T, other[1]),
        product(own[2].T, own[3]) + product(other[2].T, other[3]),
    )


def beside(high, low):
    return jnp.concatenate([high, low, jnp.zeros_like(high)], axis=-2)


def parts_to_sum(big, small):
    devices = lax.axis_size("expert") * lax.axis_size("dp")
    feature = small.shape[1]
    share = 2 * feature // devices
    lanes = 128
    flat = small.reshape(-1)
    per_device = -(-flat.shape[0] // (devices * lanes))
    flat = jnp.pad(flat, (0, devices * per_device * lanes - flat.shape[0]))
    blocks = jnp.pad(
        flat.reshape(devices, per_device, lanes), ((0, 0), (0, 8 - per_device), (0, 0))
    )

    return jnp.concatenate(
        [
            jnp.concatenate(big).astype(jnp.bfloat16).reshape(devices, share, feature),
            beside(*in_two(blocks)),
        ],
        axis=2,
    )


def add_up(arrived):
    feature = arrived.shape[2] - 128
    arrived = jnp.sum(arrived.astype(jnp.float32), axis=0)
    sums = beside(*in_two(arrived[:8, feature:] + arrived[8:16, feature:]))
    mine = jnp.concatenate([arrived[:, :feature].astype(jnp.bfloat16), sums], axis=1)
    return mine


def sums_of(everyone, count):
    feature = everyone.shape[2] - 128
    per_device = -(-count * feature // (everyone.shape[0] * 128))
    total = everyone[:, :, :feature].reshape(2 * feature, feature)
    pairs = everyone[:, :, feature:].astype(jnp.float32)
    flat = (pairs[:, :per_device] + pairs[:, 8 : 8 + per_device]).reshape(-1)
    return total[:feature], total[feature:], flat[: count * feature].reshape(count, feature)


def on_device(
    section_ends,
    routes,
    query_weight,
    key_weight,
    value_weight,
    out_weight,
    query_bias,
    value_bias,
    out_bias,
    attention_gain,
    mixture_gain,
    router_weight,
    expert_in,
    expert_down,
):
    section_id = lax.axis_index("section")
    first = section_id == 0

    def both(own):
        return own, swap(own)

    feature = section_ends.shape[2]
    row_count = section_ends.shape[1] // MICRO
    experts = router_weight.shape[2]
    holders = lax.axis_size("dp")
    devices = lax.axis_size("expert") * holders

    def my_micro(blocks):
        blocks = blocks.reshape((MICRO, row_count) + blocks.shape[1:])
        own = lax.dynamic_index_in_dim(blocks, section_id, 0, keepdims=False)
        other = swap(lax.dynamic_index_in_dim(blocks, 1 - section_id, 0, keepdims=False))
        return jnp.where(first, own, other), jnp.where(first, other, own)

    ends = both(section_ends[0])
    route_cols = my_micro(routes[0, :, 0])
    own_weights = (query_weight[0], key_weight[0], value_weight[0], out_weight[0])
    weights = (own_weights, tuple(swap(member) for member in own_weights))
    picks = (section_id.astype(jnp.int32)[None], (1 - section_id).astype(jnp.int32)[None])
    vectors = both(
        jnp.concatenate(
            [
                query_bias,
                value_bias,
                out_bias,
                attention_gain,
                mixture_gain,
                jnp.zeros((3, feature), jnp.float32),
            ]
        )
    )
    routers = both(router_weight[0])
    onehots, codes = [], []
    position = jnp.arange(row_count)
    for col in route_cols:
        same = col[:, None] == col[None, :]
        rank = jnp.sum(same & (position[None, :] < position[:, None]), axis=1)
        codes.append(col * SLOTS + rank)
        onehots.append((col[:, None] == jnp.arange(experts)[None, :]).astype(jnp.float32))
    row = jnp.arange(devices * SLOTS)
    places0 = row // (holders * SLOTS) * SLOTS + row % SLOTS
    tokens0 = codes[0]
    row = jnp.arange(experts * BLOCK)
    apart = experts * SLOTS
    places1 = row // BLOCK * SLOTS + row % TAKEN + row % BLOCK // TAKEN * apart
    row = jnp.arange(experts * BLOCK)
    half = experts * TAKEN
    source = row % half // TAKEN * BLOCK + row % TAKEN + row // half * TAKEN
    order = (source[:, None] == row[None, :]).astype(jnp.bfloat16)
    places2 = jnp.arange(experts * SLOTS)
    tokens1 = jnp.concatenate([codes[1], codes[1] + apart])
    scatters = [
        (places[:, None] == tokens[None, :]).astype(jnp.bfloat16)
        for places, tokens in ((places0, tokens0), (places1, tokens1), (places2, tokens0))
    ]
    gathers = [
        (tokens[:, None] == places[None, :]).astype(jnp.bfloat16)
        for places, tokens in ((places0, tokens0), (places1, tokens1), (places2, tokens0))
    ]
    counts = jnp.concatenate([jnp.sum(onehot, axis=0) for onehot in onehots])
    token_total = devices * row_count
    count_row = jnp.pad(counts, (0, feature - 2 * experts))[None]

    low, full = jnp.bfloat16, jnp.float32
    block = (row_count, feature)
    kept = [
        (block, low),
        (block, low),
        (block, low),
        (block, low),
        (block, low),
        (block, full),
        (block, low),
        ((row_count, experts), full),
        ((row_count, 1), full),
    ]

    *kept0, outgoing = call(
        functools.partial(forward_kernel, False),
        picks[0],
        [*ends, count_row, onehots[0], scatters[0], *vectors, *routers],
        weights,
        kept + [((devices * SLOTS, feature), low)],
    )
    outgoing, own_in, own_down = lax.optimization_barrier(
        (outgoing, expert_in[0, 0], expert_down[0, 0])
    )
    own_experts = (own_in, own_down)
    experts_of_both = (own_experts, tuple(swap(member) for member in own_experts))
    owned_in0, owned_down0 = (
        jnp.where(first, own, other) for own, other in zip(*experts_of_both)
    )
    arrived = exchange(outgoing.reshape(devices, SLOTS, feature))
    arrived, other_in, own_down = lax.optimization_barrier(
        (arrived, experts_of_both[1][0], own_down)
    )
    early = jnp.where(first, other_in, own_down)
    late = jnp.where(first, own_down, other_in)
    early = lax.all_gather(early, "dp", axis=0)
    side = section_id.astype(jnp.int32)[None]
    shares = jnp.sum(arrived[:, -1, : 2 * experts].astype(jnp.float32), axis=0) / token_total
    shares = (shares[None, :experts], shares[None, experts:])
    rows0 = arrived.reshape(devices * SLOTS, feature)
    pre0, act0, partial = expert_forward(rows0, owned_in0, owned_down0)
    returned = exchange(partial.reshape(devices, SLOTS, feature)).reshape(-1, feature)
    returned, late = lax.optimization_barrier((returned, late))
    late = lax.all_gather(late, "dp", axis=0)

    combined0, result0, *kept1, outgoing = call(
        functools.partial(forward_kernel, True),
        picks[1],
        [
            *ends,
            kept0[5],
            kept0[8],
            gathers[0],
            returned,
            onehots[1],
            scatters[1],
            *vectors,
            *routers,
        ],
        weights,
        [(block, full), (block, low)] + kept + [((experts * BLOCK, feature), low)],
    )
    outgoing, early = lax.optimization_barrier((outgoing, early))
    early_other = swap(early)
    wide1 = ((early, early_other), (early_other, early))
    arrived = exchange_experts(outgoing)
    (outgoing,) = call(
        both_ways_kernel,
        side,
        [arrived, order],
        wide1,
        [((experts * BLOCK, feature), low)],
        [((experts * TAKEN, feature), low)] * 2,
    )
    returned = exchange_experts(outgoing)
    all_rows1 = lax.all_gather(arrived, "dp", axis=0, tiled=True)
    gradients = [
        (block, low),
        (block, low),
        (block, low),
        (block, low),
        (block, low),
        ((8 + experts, feature), full),
    ]
    result1, grad_input1, *grads1, small1, outgoing = call(
        functools.partial(backward_kernel, True),
        picks[1],
        [
            *ends,
            gathers[1],
            returned,
            result0,
            kept0[8],
            scatters[2],
            *kept1,
            onehots[1],
            shares[1],
            *vectors,
            *routers,
        ],
        weights,
        [(block, low)] + gradients + [((experts * SLOTS, feature), low)],
    )
    dense_rows1 = (kept1[0], *grads1[:3], kept1[4], grads1[3])
    parts1 = parts_to_sum(dense_gradients(dense_rows1, first), small1)

    outgoing, late = lax.optimization_barrier((outgoing, late))
    late_other = swap(late)
    wide0 = ((late_other, late), (late, late_other))
    grad_rows0 = exchange_experts(outgoing)
    here = lax.dynamic_index_in_dim(
        rows0.reshape(experts, holders, SLOTS, feature),
        lax.axis_index("dp"),
        1,
        keepdims=False,
    ).reshape(-1, feature)
    (outgoing,) = call(
        back_kernel, side, [here, grad_rows0], wide0, [((experts * SLOTS, feature), low)]
    )
    returned = exchange_experts(outgoing)
    returned, parts1, all_rows1 = lax.optimization_barrier((returned, parts1, all_rows1))
    shares1 = add_up(exchange(parts1))
    gathered = lax.all_gather(grad_rows0, "dp", axis=0)
    grad_input0, *grads0, small0 = call(
        functools.partial(backward_kernel, False),
        picks[0],
        [
            *ends,
            gathers[2],
            returned,
            grad_input1,
            combined0,
            *kept0,
            onehots[0],
            shares[0],
            *vectors,
            *routers,
        ],
        weights,
        gradients,
    )
    dense_rows0 = (kept0[0], *grads0[:3], kept0[4], grads0[3])

    def own_and_other(layer0, layer1):
        own = jnp.where(first, layer0, layer1)
        return own, swap(jnp.where(first, layer1, layer0))

    def in_order(own, other):
        return jnp.where(first, jnp.stack([own, other]), jnp.stack([other, own]))

    parts0 = parts_to_sum(dense_gradients(dense_rows0, first), small0)
    parts0, shares1 = lax.optimization_barrier((parts0, shares1))
    gathered = gathered.reshape(holders, experts, SLOTS, feature).swapaxes(0, 1)
    in_grad0, down_grad0 = expert_gradients(
        rows0, pre0, act0, gathered.reshape(-1, feature), owned_down0
    )
    rows1, grad_rows1, act1, grad_pre1 = call(
        slice_kernel,
        picks[1],
        [all_rows1, order],
        experts_of_both,
        [((devices * TAKEN, feature), low)] * 4,
    )
    in_grad1 = product(rows1.T, grad_pre1)
    down_grad1 = product(act1.T, grad_rows1)
    mine = jnp.concatenate([add_up(exchange(parts0)), shares1], axis=0)
    everyone = exchange(jnp.broadcast_to(mine[None], (devices,) + mine.shape))
    count = small0.shape[0]
    length = shares1.shape[0]
    sums0 = sums_of(everyone[:, :length], count)
    sums1 = sums_of(everyone[:, length:], count)
    own, other = [], []
    for layer0, layer1 in zip(sums0, sums1):
        pair = own_and_other(layer0, layer1)
        own.append(pair[0])
        other.append(pair[1])
    dense_sums = [
        jnp.where(first, mine, theirs).astype(jnp.float32)
        for mine, theirs in (
            (own[0], other[0]),
            (own[1], other[1]),
            (other[0], own[0]),
            (other[1], own[1]),
        )
    ]
    small = own[2] + other[2]
    statistics = in_order(own[2][5:7, :experts], other[2][5:7, :experts]) / token_total
    balances = experts * jnp.sum(statistics[:, 0] * statistics[:, 1], axis=1)

    outputs = in_order(*own_and_other(result0, result1))
    grads_in = in_order(*own_and_other(grad_input0, grad_input1))
    in_own, in_other = own_and_other(in_grad0, in_grad1)
    down_own, down_other = own_and_other(down_grad0, down_grad1)
    return (
        outputs.reshape(1, -1, feature),
        grads_in.reshape(1, -1, feature),
        balances[None],
        dense_sums[0][None],
        dense_sums[1][None],
        dense_sums[2][None],
        dense_sums[3][None],
        small[0][None],
        small[1][None],
        small[2][None],
        small[3][None],
        small[4][None],
        small[8 : 8 + experts].T[None],
        (in_own + in_other)[None, None],
        (down_own + down_other)[None, None],
    )


def solution(mesh):
    placed = (
        P("section", ("expert", "dp"), None),
        P("section", ("expert", "dp"), None),
        P("section", None, None),
        P("section", None, None),
        P("section", None, None),
        P("section", None, None),
        P("section", None),
        P("section", None),
        P("section", None),
        P("section", None),
        P("section", None),
        P("section", None, None),
        P("section", "expert", None, "dp"),
        P("section", "expert", "dp", None),
    )
    return jax.shard_map(
        on_device,
        mesh=mesh,
        in_specs=placed,
        out_specs=(
            P("section", ("expert", "dp"), None),
            P("section", ("expert", "dp"), None),
            P("section", None),
            P("section", None, None),
            P("section", None, None),
            P("section", None, None),
            P("section", None, None),
            P("section", None),
            P("section", None),
            P("section", None),
            P("section", None),
            P("section", None),
            P("section", None, None),
            P("section", "expert", None, "dp"),
            P("section", "expert", "dp", None),
        ),
        check_vma=False,
    )
```

```python
import functools

import jax
import jax.numpy as jnp
from jax import lax
from jax.experimental import pallas as pl
from jax.experimental.pallas import tpu as pltpu
from jax.sharding import PartitionSpec as P

HEADS = 12
HEAD_DIM = 64
SEQ = 128
MICRO = 2
SLOTS = 16
TAKEN = 12
BLOCK = 2 * TAKEN


balance_factor = 20.0
epsilon = 1e-06
highest = lax.Precision.HIGHEST


tokens_over = ("expert", "dp")


def swap(block):
    return lax.ppermute(block, "section", [(0, 1), (1, 0)])


def exchange(block):
    return lax.all_to_all(block, tokens_over, split_axis=0, concat_axis=0, tiled=True)


def exchange_experts(block):
    feature = block.shape[1]
    experts = lax.axis_size("expert")
    parts = block.reshape(experts, -1, feature)
    arrived = lax.all_to_all(parts, "expert", split_axis=0, concat_axis=0, tiled=True)
    return arrived.reshape(-1, feature)


def rms_scale(tensor):
    return lax.rsqrt(jnp.mean(tensor * tensor, axis=-1, keepdims=True) + epsilon)


def product(left, right):
    return jnp.dot(left, right, preferred_element_type=jnp.float32)


def _nt(left, right):
    return lax.dot_general(
        left, right, (((1,), (1,)), ((), ())), preferred_element_type=jnp.float32
    )


def _tn(left, right):
    return lax.dot_general(
        left, right, (((0,), (0,)), ((), ())), preferred_element_type=jnp.float32
    )


def _split(tensor):
    high = tensor.astype(jnp.bfloat16)
    return high, (tensor - high.astype(jnp.float32)).astype(jnp.bfloat16)


def _fetch(pick_ref, sources, held, sems):
    own, other = sources
    for choice, group in ((0, own), (1, other)):

        @pl.when(pick_ref[0] == choice)
        def _():
            for i, ref in enumerate(group):
                pltpu.make_async_copy(ref, held.at[i], sems.at[i]).start()


def _arrive(sources, held, sems, i):
    pltpu.make_async_copy(sources[0][i], held.at[i], sems.at[i]).wait()


def _head_masks(rows):
    lane = lax.broadcasted_iota(jnp.int32, (rows, 2 * HEAD_DIM), 1)
    even = (lane < HEAD_DIM).astype(jnp.float32).astype(jnp.bfloat16)
    return lane < HEAD_DIM, (even, 1.0 - even)


def _chosen(pick_ref, own_ref, other_ref):
    return jnp.where(pick_ref[0] == 0, own_ref[...], other_ref[...])


def _micro_of_layer(later, pick_ref, own_ref, other_ref):
    rows = own_ref.shape[0] // MICRO
    if later:
        return jnp.where(pick_ref[0] == 0, own_ref[rows:, :], other_ref[:rows, :])
    return jnp.where(pick_ref[0] == 0, own_ref[:rows, :], other_ref[rows:, :])


def forward_kernel(later, *refs):
    refs = list(refs)
    pick_ref = refs.pop(0)
    own_ends, other_ends = refs[:2]
    refs = refs[2:]
    if later:
        hidden_in, gate_in, gather_in, returned_in = refs[:4]
        refs = refs[4:]
    else:
        count_ref = refs.pop(0)
    onehot, scatter, *sides = refs[:6]
    vectors = _chosen(pick_ref, *sides[:2])
    router = _chosen(pick_ref, *sides[2:])
    refs = refs[6:]
    own, other = refs[:4], refs[4:8]
    refs = refs[8:]
    if later:
        combined_out, result_out = refs[:2]
        refs = refs[2:]
    (
        normed_out,
        queries_out,
        keys_out,
        values_out,
        attended_out,
        hidden_out,
        moe_out,
        probs_out,
        gate_out,
        outgoing,
        held,
        sems,
    ) = refs
    weights = (own, other)
    _fetch(pick_ref, weights, held, sems)
    if later:
        combined = product(gather_in[...], returned_in[...])
        combined_out[...] = combined
        low = (hidden_in[...] + gate_in[...] * combined).astype(jnp.bfloat16)
        result_out[...] = low
        inputs = low.astype(jnp.float32)
    else:
        inputs = _micro_of_layer(later, pick_ref, own_ends, other_ends).astype(jnp.float32)
    rows = inputs.shape[0]
    normed = (inputs * rms_scale(inputs) * vectors[3:4, :]).astype(jnp.bfloat16)
    normed_out[...] = normed
    _arrive(weights, held, sems, 0)
    queries_out[...] = (product(normed, held[0]) + vectors[0:1, :]).astype(jnp.bfloat16)
    _arrive(weights, held, sems, 1)
    keys_out[...] = product(normed, held[1]).astype(jnp.bfloat16)
    _arrive(weights, held, sems, 2)
    values_out[...] = (product(normed, held[2]) + vectors[1:2, :]).astype(jnp.bfloat16)
    first_half, masks = _head_masks(rows)
    scaling = HEAD_DIM ** (-0.5)
    for pair in range(HEADS // 2):
        lanes = slice(2 * HEAD_DIM * pair, 2 * HEAD_DIM * (pair + 1))
        query, key, value = queries_out[:, lanes], keys_out[:, lanes], values_out[:, lanes]
        parts = []
        for mask in masks:
            scores = _nt(query * mask, key) * scaling
            shifted = jnp.exp(scores - jnp.max(scores, axis=-1, keepdims=True))
            weight = shifted / jnp.sum(shifted, axis=-1, keepdims=True)
            parts.append(product(weight.astype(jnp.bfloat16), value))
        attended_out[:, lanes] = jnp.where(first_half, parts[0], parts[1]).astype(jnp.bfloat16)
    _arrive(weights, held, sems, 3)
    hidden = inputs + product(attended_out[...], held[3]) + vectors[2:3, :]
    hidden_out[...] = hidden
    moe = (hidden * rms_scale(hidden) * vectors[4:5, :]).astype(jnp.bfloat16)
    moe_out[...] = moe
    logits = product(moe, router)
    shifted = jnp.exp(logits - jnp.max(logits, axis=-1, keepdims=True))
    probs = shifted / jnp.sum(shifted, axis=-1, keepdims=True)
    probs_out[...] = probs
    gate = jnp.sum(probs * onehot[...], axis=-1, keepdims=True)
    gate_out[...] = gate
    if later:
        cotangent = _micro_of_layer(later, pick_ref, own_ends, other_ends)
        grad_tokens = (gate * cotangent.astype(jnp.float32)).astype(jnp.bfloat16)
        outgoing[...] = product(
            scatter[...], jnp.concatenate([moe, grad_tokens], axis=0)
        ).astype(jnp.bfloat16)
    else:
        slots = product(scatter[...], moe)
        row = lax.broadcasted_iota(jnp.int32, slots.shape, 0)
        outgoing[...] = jnp.where(row % SLOTS == SLOTS - 1, count_ref[...], slots).astype(
            jnp.bfloat16
        )


def backward_kernel(later, *refs):
    refs = list(refs)
    pick_ref = refs.pop(0)
    own_ends, other_ends, gather_in, returned_in, *refs = refs
    ends = _micro_of_layer(later, pick_ref, own_ends, other_ends)
    if later:
        grad_result = ends.astype(jnp.float32)
        inputs_in = refs.pop(0)
        next_gate, next_scatter, *refs = refs
    else:
        grad_in = refs.pop(0)
        grad_result = grad_in[...].astype(jnp.float32)
        combined_in = refs.pop(0)
        inputs_in = ends
    (
        normed_in,
        queries_in,
        keys_in,
        values_in,
        attended_in,
        hidden_in,
        moe_in,
        probs_in,
        gate_in,
        onehot_in,
        share_in,
        *refs,
    ) = refs
    vectors = _chosen(pick_ref, *refs[:2])
    router = _chosen(pick_ref, *refs[2:4])
    refs = refs[4:]
    weights = (refs[:4], refs[4:8])
    refs = refs[8:]
    if later:
        result_out = refs.pop(0)
    (
        dx_out,
        dq_out,
        dk_out,
        dv_out,
        da_out,
        small_out,
        *refs,
    ) = refs
    if later:
        next_outgoing = refs.pop(0)
    held, sems = refs
    _fetch(pick_ref, weights, held, sems)
    rows, feature = grad_result.shape
    hidden = hidden_in[...]
    back = product(gather_in[...], returned_in[...])
    if later:
        combined, grad_normed = back[:rows], back[rows:]
        result_out[...] = (hidden + gate_in[...] * combined).astype(jnp.bfloat16)
    else:
        combined, grad_normed = combined_in[...], back
    probs = probs_in[...]
    onehot = onehot_in[...]
    experts = onehot.shape[1]
    grad_gate = jnp.sum(grad_result * combined, axis=-1, keepdims=True)
    grad_probs = onehot * grad_gate + balance_factor * experts * share_in[...]
    grad_logits = probs * (grad_probs - jnp.sum(probs * grad_probs, axis=-1, keepdims=True))
    high, low = _split(grad_logits)
    small_out[8 : 8 + experts, :] = _tn(high, moe_in[...]) + _tn(low, moe_in[...])
    grad_normed = grad_normed + _nt(high, router) + _nt(low, router)
    scale = rms_scale(hidden)
    mixture_grad = jnp.sum(grad_normed * hidden * scale, axis=0, keepdims=True)
    grad_scaled = grad_normed * vectors[4:5, :]
    grad_hidden = (
        grad_result
        + scale * grad_scaled
        - hidden * (scale * scale * scale) * jnp.mean(grad_scaled * hidden, axis=-1, keepdims=True)
    )
    branch = grad_hidden.astype(jnp.bfloat16)
    da_out[...] = branch
    out_bias_grad = jnp.sum(branch.astype(jnp.float32), axis=0, keepdims=True)
    _arrive(weights, held, sems, 3)
    grad_attended = _nt(branch, held[3]).astype(jnp.bfloat16)
    first_half, masks = _head_masks(rows)
    scaling = HEAD_DIM ** (-0.5)
    for pair in range(HEADS // 2):
        lanes = slice(2 * HEAD_DIM * pair, 2 * HEAD_DIM * (pair + 1))
        query, key, value = queries_in[:, lanes], keys_in[:, lanes], values_in[:, lanes]
        grad = grad_attended[:, lanes]
        parts = []
        for mask in masks:
            scores = _nt(query * mask, key) * scaling
            shifted = jnp.exp(scores - jnp.max(scores, axis=-1, keepdims=True))
            weight = shifted / jnp.sum(shifted, axis=-1, keepdims=True)
            grad_weight = _nt(grad * mask, value)
            delta = jnp.sum(weight * grad_weight, axis=-1, keepdims=True)
            grad_score = (weight * (grad_weight - delta)).astype(jnp.bfloat16)
            parts.append(
                (
                    product(grad_score, key) * scaling,
                    _tn(grad_score, query) * scaling,
                    _tn(weight.astype(jnp.bfloat16), grad),
                )
            )
        for out, left, right in zip((dq_out, dk_out, dv_out), *parts):
            out[:, lanes] = jnp.where(first_half, left, right).astype(jnp.bfloat16)
    _arrive(weights, held, sems, 0)
    _arrive(weights, held, sems, 1)
    _arrive(weights, held, sems, 2)
    grad_first = _nt(dq_out[...], held[0]) + _nt(dk_out[...], held[1]) + _nt(dv_out[...], held[2])
    inputs = inputs_in[...].astype(jnp.float32)
    scale = rms_scale(inputs)
    attention_grad = jnp.sum(grad_first * inputs * scale, axis=0, keepdims=True)
    grad_scaled = grad_first * vectors[3:4, :]
    dx_out[...] = (
        grad_hidden
        + scale * grad_scaled
        - inputs * (scale * scale * scale) * jnp.mean(grad_scaled * inputs, axis=-1, keepdims=True)
    ).astype(jnp.bfloat16)
    small_out[0:1, :] = jnp.sum(dq_out[...].astype(jnp.float32), axis=0, keepdims=True)
    small_out[1:2, :] = jnp.sum(dv_out[...].astype(jnp.float32), axis=0, keepdims=True)
    small_out[2:3, :] = out_bias_grad
    small_out[3:4, :] = attention_grad
    small_out[4:5, :] = mixture_grad
    small_out[5:8, :] = jnp.zeros((3, feature), jnp.float32)
    small_out[5:6, :experts] = jnp.sum(onehot, axis=0, keepdims=True)
    small_out[6:7, :experts] = jnp.sum(probs, axis=0, keepdims=True)
    if later:
        grad_tokens = (next_gate[...] * dx_out[...].astype(jnp.float32)).astype(jnp.bfloat16)
        next_outgoing[...] = product(next_scatter[...], grad_tokens).astype(jnp.bfloat16)


def call(kernel, pick, arrays, weights, outs, scratch=()):
    def whole(shape):
        return pl.BlockSpec(shape, lambda i: (0,) * len(shape), pipeline_mode=pl.Buffered(1))

    anywhere = pl.BlockSpec(memory_space=pl.ANY)
    own, other = weights
    return pl.pallas_call(
        kernel,
        out_shape=[jax.ShapeDtypeStruct(shape, dtype) for shape, dtype in outs],
        grid=(1,),
        in_specs=[pl.BlockSpec(memory_space=pltpu.SMEM)]
        + [whole(array.shape) for array in arrays]
        + [anywhere] * (len(own) + len(other)),
        out_specs=[whole(shape) for shape, dtype in outs],
        scratch_shapes=[pltpu.VMEM(shape, dtype) for shape, dtype in scratch]
        + [
            pltpu.VMEM((len(own),) + own[0].shape, own[0].dtype),
            pltpu.SemaphoreType.DMA((len(own),) + own[0].shape[:-2]),
        ],
        compiler_params=pltpu.CompilerParams(vmem_limit_bytes=58 * 1024 * 1024),
    )(pick, *arrays, *own, *other)


def gelu_parts(pre):
    root = 0.7978845608028654
    square = pre * pre
    bend = jnp.tanh(root * (pre + 0.044715 * square * pre))
    slope = 0.5 * (1.0 + bend) + (0.5 * root) * pre * (1.0 - bend * bend) * (
        1.0 + 3 * 0.044715 * square
    )
    return 0.5 * pre * (1.0 + bend), slope


def sort_apart(order, mixed, rows_out, grads_out):
    group = order.shape[0]
    half = group // 2
    for i in range(mixed.shape[0] // group):
        apart = product(order[...], mixed[group * i : group * (i + 1), :]).astype(jnp.bfloat16)
        rows_out[half * i : half * (i + 1), :] = apart[:half]
        grads_out[half * i : half * (i + 1), :] = apart[half:]


def slice_kernel(
    pick_ref,
    mixed,
    order,
    own_in,
    own_down,
    other_in,
    other_down,
    rows_out,
    grads_out,
    act_out,
    grad_pre_out,
    held,
    sems,
):
    weights = ((own_in, own_down), (other_in, other_down))
    _fetch(pick_ref, weights, held, sems)
    sort_apart(order, mixed, rows_out, grads_out)
    _arrive(weights, held, sems, 0)
    act, slope = gelu_parts(product(rows_out[...], held[0]))
    act_out[...] = act.astype(jnp.bfloat16)
    _arrive(weights, held, sems, 1)
    grad_pre_out[...] = (slope * _nt(grads_out[...], held[1])).astype(jnp.bfloat16)


def _fetch_wide(pick_ref, weights, held, sems):
    for choice in (0, 1):

        @pl.when(pick_ref[0] == choice)
        def _():
            for part in range(held.shape[1]):
                for i, ref in enumerate(weights[choice]):
                    pltpu.make_async_copy(
                        ref.at[part], held.at[i, part], sems.at[i, part]
                    ).start()


def _arrive_wide(weights, held, sems, part):
    for i, ref in enumerate(weights[0]):
        pltpu.make_async_copy(ref.at[part], held.at[i, part], sems.at[i, part]).wait()


def both_ways_kernel(
    pick_ref, mixed, order, own_in, own_down, other_in, other_down, outgoing, rows, grads, held, sems
):
    weights = ((own_in, own_down), (other_in, other_down))
    _fetch_wide(pick_ref, weights, held, sems)
    sort_apart(order, mixed, rows, grads)
    total = jnp.zeros(rows.shape, jnp.float32)
    grad_total = jnp.zeros(rows.shape, jnp.float32)
    for part in range(held.shape[1]):
        _arrive_wide(weights, held, sems, part)
        act, slope = gelu_parts(product(rows[...], held[0, part]))
        total = total + product(act.astype(jnp.bfloat16), held[1, part])
        grad_pre = (slope * _nt(grads[...], held[1, part])).astype(jnp.bfloat16)
        grad_total = grad_total + _nt(grad_pre, held[0, part])
    apart = jnp.concatenate([total.astype(jnp.bfloat16), grad_total.astype(jnp.bfloat16)], axis=0)
    outgoing[...] = _tn(order[...], apart).astype(jnp.bfloat16)


def back_kernel(
    pick_ref, rows, grads, own_in, own_down, other_in, other_down, outgoing, held, sems
):
    weights = ((own_in, own_down), (other_in, other_down))
    _fetch_wide(pick_ref, weights, held, sems)
    grad_total = jnp.zeros(rows.shape, jnp.float32)
    for part in range(held.shape[1]):
        _arrive_wide(weights, held, sems, part)
        act, slope = gelu_parts(product(rows[...], held[0, part]))
        grad_pre = (slope * _nt(grads[...], held[1, part])).astype(jnp.bfloat16)
        grad_total = grad_total + _nt(grad_pre, held[0, part])
    outgoing[...] = grad_total.astype(jnp.bfloat16)


def expert_forward(rows, owned_in, owned_down):
    pre_act = product(rows, owned_in)
    activated = jax.nn.gelu(pre_act).astype(jnp.bfloat16)
    return pre_act, activated, product(activated, owned_down).astype(jnp.bfloat16)


def expert_gradients(rows, pre_act, activated, grad_rows, owned_down):
    grad_act = product(grad_rows, owned_down.T)
    grad_pre = (gelu_parts(pre_act)[1] * grad_act).astype(jnp.bfloat16)
    return product(rows.T, grad_pre), product(activated.T, grad_rows)


def in_two(tensor):
    high = lax.reduce_precision(tensor, 8, 7)
    return high.astype(jnp.bfloat16), (tensor - high).astype(jnp.bfloat16)


def dense_gradients(rows, first):
    normed, grad_queries, grad_keys, grad_values, attended, grad_branch = rows

    def pick(left, right):
        return jnp.where(first, left, right)

    own = (
        normed,
        pick(grad_queries, grad_values),
        pick(normed, attended),
        pick(grad_keys, grad_branch),
    )
    other = (
        swap(normed),
        swap(pick(grad_values, grad_queries)),
        swap(pick(attended, normed)),
        swap(pick(grad_branch, grad_keys)),
    )
    return (
        product(own[0].T, own[1]) + product(other[0].T, other[1]),
        product(own[2].T, own[3]) + product(other[2].T, other[3]),
    )


def beside(high, low):
    return jnp.concatenate([high, low, jnp.zeros_like(high)], axis=-2)


def parts_to_sum(big, small):
    devices = lax.axis_size("expert") * lax.axis_size("dp")
    feature = small.shape[1]
    share = 2 * feature // devices
    lanes = 128
    flat = small.reshape(-1)
    per_device = -(-flat.shape[0] // (devices * lanes))
    flat = jnp.pad(flat, (0, devices * per_device * lanes - flat.shape[0]))
    blocks = jnp.pad(
        flat.reshape(devices, per_device, lanes), ((0, 0), (0, 8 - per_device), (0, 0))
    )

    return jnp.concatenate(
        [
            jnp.concatenate(big).astype(jnp.bfloat16).reshape(devices, share, feature),
            beside(*in_two(blocks)),
        ],
        axis=2,
    )


def add_up(arrived):
    feature = arrived.shape[2] - 128
    arrived = jnp.sum(arrived.astype(jnp.float32), axis=0)
    sums = beside(*in_two(arrived[:8, feature:] + arrived[8:16, feature:]))
    mine = jnp.concatenate([arrived[:, :feature].astype(jnp.bfloat16), sums], axis=1)
    return mine


def sums_of(everyone, count):
    feature = everyone.shape[2] - 128
    per_device = -(-count * feature // (everyone.shape[0] * 128))
    total = everyone[:, :, :feature].reshape(2 * feature, feature)
    pairs = everyone[:, :, feature:].astype(jnp.float32)
    flat = (pairs[:, :per_device] + pairs[:, 8 : 8 + per_device]).reshape(-1)
    return total[:feature], total[feature:], flat[: count * feature].reshape(count, feature)


def on_device(
    section_ends,
    routes,
    query_weight,
    key_weight,
    value_weight,
    out_weight,
    query_bias,
    value_bias,
    out_bias,
    attention_gain,
    mixture_gain,
    router_weight,
    expert_in,
    expert_down,
):
    section_id = lax.axis_index("section")
    first = section_id == 0

    def both(own):
        return own, swap(own)

    feature = section_ends.shape[2]
    row_count = section_ends.shape[1] // MICRO
    experts = router_weight.shape[2]
    holders = lax.axis_size("dp")
    devices = lax.axis_size("expert") * holders

    def my_micro(blocks):
        blocks = blocks.reshape((MICRO, row_count) + blocks.shape[1:])
        own = lax.dynamic_index_in_dim(blocks, section_id, 0, keepdims=False)
        other = swap(lax.dynamic_index_in_dim(blocks, 1 - section_id, 0, keepdims=False))
        return jnp.where(first, own, other), jnp.where(first, other, own)

    ends = both(section_ends[0])
    route_cols = my_micro(routes[0, :, 0])
    own_weights = (query_weight[0], key_weight[0], value_weight[0], out_weight[0])
    weights = (own_weights, tuple(swap(member) for member in own_weights))
    picks = (section_id.astype(jnp.int32)[None], (1 - section_id).astype(jnp.int32)[None])
    vectors = both(
        jnp.concatenate(
            [
                query_bias,
                value_bias,
                out_bias,
                attention_gain,
                mixture_gain,
                jnp.zeros((3, feature), jnp.float32),
            ]
        )
    )
    routers = both(router_weight[0])
    onehots, codes = [], []
    position = jnp.arange(row_count)
    for col in route_cols:
        same = col[:, None] == col[None, :]
        rank = jnp.sum(same & (position[None, :] < position[:, None]), axis=1)
        codes.append(col * SLOTS + rank)
        onehots.append((col[:, None] == jnp.arange(experts)[None, :]).astype(jnp.float32))
    row = jnp.arange(devices * SLOTS)
    places0 = row // (holders * SLOTS) * SLOTS + row % SLOTS
    tokens0 = codes[0]
    row = jnp.arange(experts * BLOCK)
    apart = experts * SLOTS
    places1 = row // BLOCK * SLOTS + row % TAKEN + row % BLOCK // TAKEN * apart
    row = jnp.arange(experts * BLOCK)
    half = experts * TAKEN
    source = row % half // TAKEN * BLOCK + row % TAKEN + row // half * TAKEN
    order = (source[:, None] == row[None, :]).astype(jnp.bfloat16)
    places2 = jnp.arange(experts * SLOTS)
    tokens1 = jnp.concatenate([codes[1], codes[1] + apart])
    scatters = [
        (places[:, None] == tokens[None, :]).astype(jnp.bfloat16)
        for places, tokens in ((places0, tokens0), (places1, tokens1), (places2, tokens0))
    ]
    gathers = [
        (tokens[:, None] == places[None, :]).astype(jnp.bfloat16)
        for places, tokens in ((places0, tokens0), (places1, tokens1), (places2, tokens0))
    ]
    counts = jnp.concatenate([jnp.sum(onehot, axis=0) for onehot in onehots])
    token_total = devices * row_count
    count_row = jnp.pad(counts, (0, feature - 2 * experts))[None]

    low, full = jnp.bfloat16, jnp.float32
    block = (row_count, feature)
    kept = [
        (block, low),
        (block, low),
        (block, low),
        (block, low),
        (block, low),
        (block, full),
        (block, low),
        ((row_count, experts), full),
        ((row_count, 1), full),
    ]

    *kept0, outgoing = call(
        functools.partial(forward_kernel, False),
        picks[0],
        [*ends, count_row, onehots[0], scatters[0], *vectors, *routers],
        weights,
        kept + [((devices * SLOTS, feature), low)],
    )
    outgoing, own_in, own_down = lax.optimization_barrier(
        (outgoing, expert_in[0, 0], expert_down[0, 0])
    )
    own_experts = (own_in, own_down)
    experts_of_both = (own_experts, tuple(swap(member) for member in own_experts))
    owned_in0, owned_down0 = (
        jnp.where(first, own, other) for own, other in zip(*experts_of_both)
    )
    arrived = exchange(outgoing.reshape(devices, SLOTS, feature))
    arrived, other_in, own_down = lax.optimization_barrier(
        (arrived, experts_of_both[1][0], own_down)
    )
    early = jnp.where(first, other_in, own_down)
    late = jnp.where(first, own_down, other_in)
    early = lax.all_gather(early, "dp", axis=0)
    side = section_id.astype(jnp.int32)[None]
    shares = jnp.sum(arrived[:, -1, : 2 * experts].astype(jnp.float32), axis=0) / token_total
    shares = (shares[None, :experts], shares[None, experts:])
    rows0 = arrived.reshape(devices * SLOTS, feature)
    pre0, act0, partial = expert_forward(rows0, owned_in0, owned_down0)
    returned = exchange(partial.reshape(devices, SLOTS, feature)).reshape(-1, feature)
    returned, late = lax.optimization_barrier((returned, late))
    late = lax.all_gather(late, "dp", axis=0)

    combined0, result0, *kept1, outgoing = call(
        functools.partial(forward_kernel, True),
        picks[1],
        [
            *ends,
            kept0[5],
            kept0[8],
            gathers[0],
            returned,
            onehots[1],
            scatters[1],
            *vectors,
            *routers,
        ],
        weights,
        [(block, full), (block, low)] + kept + [((experts * BLOCK, feature), low)],
    )
    outgoing, early = lax.optimization_barrier((outgoing, early))
    early_other = swap(early)
    wide1 = ((early, early_other), (early_other, early))
    arrived = exchange_experts(outgoing)
    (outgoing,) = call(
        both_ways_kernel,
        side,
        [arrived, order],
        wide1,
        [((experts * BLOCK, feature), low)],
        [((experts * TAKEN, feature), low)] * 2,
    )
    returned = exchange_experts(outgoing)
    all_rows1 = lax.all_gather(arrived, "dp", axis=0, tiled=True)
    gradients = [
        (block, low),
        (block, low),
        (block, low),
        (block, low),
        (block, low),
        ((8 + experts, feature), full),
    ]
    result1, grad_input1, *grads1, small1, outgoing = call(
        functools.partial(backward_kernel, True),
        picks[1],
        [
            *ends,
            gathers[1],
            returned,
            result0,
            kept0[8],
            scatters[2],
            *kept1,
            onehots[1],
            shares[1],
            *vectors,
            *routers,
        ],
        weights,
        [(block, low)] + gradients + [((experts * SLOTS, feature), low)],
    )
    dense_rows1 = (kept1[0], *grads1[:3], kept1[4], grads1[3])
    parts1 = parts_to_sum(dense_gradients(dense_rows1, first), small1)

    outgoing, late = lax.optimization_barrier((outgoing, late))
    late_other = swap(late)
    wide0 = ((late_other, late), (late, late_other))
    grad_rows0 = exchange_experts(outgoing)
    here = lax.dynamic_index_in_dim(
        rows0.reshape(experts, holders, SLOTS, feature),
        lax.axis_index("dp"),
        1,
        keepdims=False,
    ).reshape(-1, feature)
    (outgoing,) = call(
        back_kernel, side, [here, grad_rows0], wide0, [((experts * SLOTS, feature), low)]
    )
    returned = exchange_experts(outgoing)
    returned, parts1, all_rows1 = lax.optimization_barrier((returned, parts1, all_rows1))
    shares1 = add_up(exchange(parts1))
    gathered = lax.all_gather(grad_rows0, "dp", axis=0)
    grad_input0, *grads0, small0 = call(
        functools.partial(backward_kernel, False),
        picks[0],
        [
            *ends,
            gathers[2],
            returned,
            grad_input1,
            combined0,
            *kept0,
            onehots[0],
            shares[0],
            *vectors,
            *routers,
        ],
        weights,
        gradients,
    )
    dense_rows0 = (kept0[0], *grads0[:3], kept0[4], grads0[3])

    def own_and_other(layer0, layer1):
        own = jnp.where(first, layer0, layer1)
        return own, swap(jnp.where(first, layer1, layer0))

    def in_order(own, other):
        return jnp.where(first, jnp.stack([own, other]), jnp.stack([other, own]))

    parts0 = parts_to_sum(dense_gradients(dense_rows0, first), small0)
    parts0, shares1 = lax.optimization_barrier((parts0, shares1))
    gathered = gathered.reshape(holders, experts, SLOTS, feature).swapaxes(0, 1)
    in_grad0, down_grad0 = expert_gradients(
        rows0, pre0, act0, gathered.reshape(-1, feature), owned_down0
    )
    rows1, grad_rows1, act1, grad_pre1 = call(
        slice_kernel,
        picks[1],
        [all_rows1, order],
        experts_of_both,
        [((devices * TAKEN, feature), low)] * 4,
    )
    in_grad1 = product(rows1.T, grad_pre1)
    down_grad1 = product(act1.T, grad_rows1)
    own, other = own_and_other(add_up(exchange(parts0)), shares1)
    mine = jnp.where(
        first, jnp.concatenate([own, other], axis=0), jnp.concatenate([other, own], axis=0)
    )
    everyone = exchange(jnp.broadcast_to(mine[None], (devices,) + mine.shape))
    count = small0.shape[0]
    length = shares1.shape[0]
    query_sum, key_sum, small = sums_of(everyone[:, :length], count)
    value_sum, out_sum, other_small = sums_of(everyone[:, length:], count)
    dense_sums = [
        member.astype(jnp.float32) for member in (query_sum, key_sum, value_sum, out_sum)
    ]
    statistics = jnp.stack([small[5:7, :experts], other_small[5:7, :experts]]) / token_total
    small = small + other_small
    balances = experts * jnp.sum(statistics[:, 0] * statistics[:, 1], axis=1)

    outputs = in_order(*own_and_other(result0, result1))
    grads_in = in_order(*own_and_other(grad_input0, grad_input1))
    in_own, in_other = own_and_other(in_grad0, in_grad1)
    down_own, down_other = own_and_other(down_grad0, down_grad1)
    return (
        outputs.reshape(1, -1, feature),
        grads_in.reshape(1, -1, feature),
        balances[None],
        dense_sums[0][None],
        dense_sums[1][None],
        dense_sums[2][None],
        dense_sums[3][None],
        small[0][None],
        small[1][None],
        small[2][None],
        small[3][None],
        small[4][None],
        small[8 : 8 + experts].T[None],
        (in_own + in_other)[None, None],
        (down_own + down_other)[None, None],
    )


def solution(mesh):
    placed = (
        P("section", ("expert", "dp"), None),
        P("section", ("expert", "dp"), None),
        P("section", None, None),
        P("section", None, None),
        P("section", None, None),
        P("section", None, None),
        P("section", None),
        P("section", None),
        P("section", None),
        P("section", None),
        P("section", None),
        P("section", None, None),
        P("section", "expert", None, "dp"),
        P("section", "expert", "dp", None),
    )
    return jax.shard_map(
        on_device,
        mesh=mesh,
        in_specs=placed,
        out_specs=(
            P("section", ("expert", "dp"), None),
            P("section", ("expert", "dp"), None),
            P("section", None),
            P("section", None, None),
            P("section", None, None),
            P("section", None, None),
            P("section", None, None),
            P("section", None),
            P("section", None),
            P("section", None),
            P("section", None),
            P("section", None),
            P("section", None, None),
            P("section", "expert", None, "dp"),
            P("section", "expert", "dp", None),
        ),
        check_vma=False,
    )
```

```python
import functools

import jax
import jax.numpy as jnp
from jax import lax
from jax.experimental import pallas as pl
from jax.experimental.pallas import tpu as pltpu
from jax.sharding import PartitionSpec as P

HEADS = 12
HEAD_DIM = 64
SEQ = 128
MICRO = 2
SLOTS = 16
TAKEN = 12
BLOCK = 2 * TAKEN


balance_factor = 20.0
epsilon = 1e-06
highest = lax.Precision.HIGHEST


tokens_over = ("expert", "dp")


def swap(block):
    return lax.ppermute(block, "section", [(0, 1), (1, 0)])


def exchange(block):
    return lax.all_to_all(block, tokens_over, split_axis=0, concat_axis=0, tiled=True)


def exchange_experts(block):
    feature = block.shape[1]
    experts = lax.axis_size("expert")
    parts = block.reshape(experts, -1, feature)
    arrived = lax.all_to_all(parts, "expert", split_axis=0, concat_axis=0, tiled=True)
    return arrived.reshape(-1, feature)


def rms_scale(tensor):
    return lax.rsqrt(jnp.mean(tensor * tensor, axis=-1, keepdims=True) + epsilon)


def product(left, right):
    return jnp.dot(left, right, preferred_element_type=jnp.float32)


def _nt(left, right):
    return lax.dot_general(
        left, right, (((1,), (1,)), ((), ())), preferred_element_type=jnp.float32
    )


def _tn(left, right):
    return lax.dot_general(
        left, right, (((0,), (0,)), ((), ())), preferred_element_type=jnp.float32
    )


def _split(tensor):
    high = tensor.astype(jnp.bfloat16)
    return high, (tensor - high.astype(jnp.float32)).astype(jnp.bfloat16)


def _fetch(pick_ref, sources, held, sems):
    own, other = sources
    for choice, group in ((0, own), (1, other)):

        @pl.when(pick_ref[0] == choice)
        def _():
            for i, ref in enumerate(group):
                pltpu.make_async_copy(ref, held.at[i], sems.at[i]).start()


def _arrive(sources, held, sems, i):
    pltpu.make_async_copy(sources[0][i], held.at[i], sems.at[i]).wait()


def _head_masks(rows):
    lane = lax.broadcasted_iota(jnp.int32, (rows, 2 * HEAD_DIM), 1)
    even = (lane < HEAD_DIM).astype(jnp.float32).astype(jnp.bfloat16)
    return lane < HEAD_DIM, (even, 1.0 - even)


def _chosen(pick_ref, own_ref, other_ref):
    return jnp.where(pick_ref[0] == 0, own_ref[...], other_ref[...])


def _micro_of_layer(later, pick_ref, own_ref, other_ref):
    rows = own_ref.shape[0] // MICRO
    if later:
        return jnp.where(pick_ref[0] == 0, own_ref[rows:, :], other_ref[:rows, :])
    return jnp.where(pick_ref[0] == 0, own_ref[:rows, :], other_ref[rows:, :])


def forward_kernel(later, *refs):
    refs = list(refs)
    pick_ref = refs.pop(0)
    own_ends, other_ends = refs[:2]
    refs = refs[2:]
    if later:
        hidden_in, gate_in, gather_in, returned_in = refs[:4]
        refs = refs[4:]
    else:
        count_ref = refs.pop(0)
    onehot, scatter, *sides = refs[:6]
    vectors = _chosen(pick_ref, *sides[:2])
    router = _chosen(pick_ref, *sides[2:])
    refs = refs[6:]
    own, other = refs[:4], refs[4:8]
    refs = refs[8:]
    if later:
        combined_out, result_out = refs[:2]
        refs = refs[2:]
    (
        normed_out,
        queries_out,
        keys_out,
        values_out,
        attended_out,
        hidden_out,
        moe_out,
        probs_out,
        gate_out,
        outgoing,
        held,
        sems,
    ) = refs
    weights = (own, other)
    _fetch(pick_ref, weights, held, sems)
    if later:
        combined = product(gather_in[...], returned_in[...])
        combined_out[...] = combined
        low = (hidden_in[...] + gate_in[...] * combined).astype(jnp.bfloat16)
        result_out[...] = low
        inputs = low.astype(jnp.float32)
    else:
        inputs = _micro_of_layer(later, pick_ref, own_ends, other_ends).astype(jnp.float32)
    rows = inputs.shape[0]
    normed = (inputs * rms_scale(inputs) * vectors[3:4, :]).astype(jnp.bfloat16)
    normed_out[...] = normed
    _arrive(weights, held, sems, 0)
    queries_out[...] = (product(normed, held[0]) + vectors[0:1, :]).astype(jnp.bfloat16)
    _arrive(weights, held, sems, 1)
    keys_out[...] = product(normed, held[1]).astype(jnp.bfloat16)
    _arrive(weights, held, sems, 2)
    values_out[...] = (product(normed, held[2]) + vectors[1:2, :]).astype(jnp.bfloat16)
    first_half, masks = _head_masks(rows)
    scaling = HEAD_DIM ** (-0.5)
    for pair in range(HEADS // 2):
        lanes = slice(2 * HEAD_DIM * pair, 2 * HEAD_DIM * (pair + 1))
        query, key, value = queries_out[:, lanes], keys_out[:, lanes], values_out[:, lanes]
        parts = []
        for mask in masks:
            scores = _nt(query * mask, key) * scaling
            shifted = jnp.exp(scores - jnp.max(scores, axis=-1, keepdims=True))
            weight = shifted / jnp.sum(shifted, axis=-1, keepdims=True)
            parts.append(product(weight.astype(jnp.bfloat16), value))
        attended_out[:, lanes] = jnp.where(first_half, parts[0], parts[1]).astype(jnp.bfloat16)
    _arrive(weights, held, sems, 3)
    hidden = inputs + product(attended_out[...], held[3]) + vectors[2:3, :]
    hidden_out[...] = hidden
    moe = (hidden * rms_scale(hidden) * vectors[4:5, :]).astype(jnp.bfloat16)
    moe_out[...] = moe
    logits = product(moe, router)
    shifted = jnp.exp(logits - jnp.max(logits, axis=-1, keepdims=True))
    probs = shifted / jnp.sum(shifted, axis=-1, keepdims=True)
    probs_out[...] = probs
    gate = jnp.sum(probs * onehot[...], axis=-1, keepdims=True)
    gate_out[...] = gate
    if later:
        cotangent = _micro_of_layer(later, pick_ref, own_ends, other_ends)
        grad_tokens = (gate * cotangent.astype(jnp.float32)).astype(jnp.bfloat16)
        outgoing[...] = product(
            scatter[...], jnp.concatenate([moe, grad_tokens], axis=0)
        ).astype(jnp.bfloat16)
    else:
        slots = product(scatter[...], moe)
        row = lax.broadcasted_iota(jnp.int32, slots.shape, 0)
        outgoing[...] = jnp.where(row % SLOTS == SLOTS - 1, count_ref[...], slots).astype(
            jnp.bfloat16
        )


def backward_kernel(later, *refs):
    refs = list(refs)
    pick_ref = refs.pop(0)
    own_ends, other_ends, gather_in, returned_in, *refs = refs
    ends = _micro_of_layer(later, pick_ref, own_ends, other_ends)
    if later:
        grad_result = ends.astype(jnp.float32)
        inputs_in = refs.pop(0)
        next_gate, next_scatter, *refs = refs
    else:
        grad_in = refs.pop(0)
        grad_result = grad_in[...].astype(jnp.float32)
        combined_in = refs.pop(0)
        inputs_in = ends
    (
        normed_in,
        queries_in,
        keys_in,
        values_in,
        attended_in,
        hidden_in,
        moe_in,
        probs_in,
        gate_in,
        onehot_in,
        share_in,
        *refs,
    ) = refs
    vectors = _chosen(pick_ref, *refs[:2])
    router = _chosen(pick_ref, *refs[2:4])
    refs = refs[4:]
    weights = (refs[:4], refs[4:8])
    refs = refs[8:]
    if later:
        result_out = refs.pop(0)
    (
        dx_out,
        dq_out,
        dk_out,
        dv_out,
        da_out,
        small_out,
        *refs,
    ) = refs
    if later:
        next_outgoing = refs.pop(0)
    held, sems = refs
    _fetch(pick_ref, weights, held, sems)
    rows, feature = grad_result.shape
    hidden = hidden_in[...]
    back = product(gather_in[...], returned_in[...])
    if later:
        combined, grad_normed = back[:rows], back[rows:]
        result_out[...] = (hidden + gate_in[...] * combined).astype(jnp.bfloat16)
    else:
        combined, grad_normed = combined_in[...], back
    probs = probs_in[...]
    onehot = onehot_in[...]
    experts = onehot.shape[1]
    grad_gate = jnp.sum(grad_result * combined, axis=-1, keepdims=True)
    grad_probs = onehot * grad_gate + balance_factor * experts * share_in[...]
    grad_logits = probs * (grad_probs - jnp.sum(probs * grad_probs, axis=-1, keepdims=True))
    high, low = _split(grad_logits)
    small_out[8 : 8 + experts, :] = _tn(high, moe_in[...]) + _tn(low, moe_in[...])
    grad_normed = grad_normed + _nt(high, router) + _nt(low, router)
    scale = rms_scale(hidden)
    mixture_grad = jnp.sum(grad_normed * hidden * scale, axis=0, keepdims=True)
    grad_scaled = grad_normed * vectors[4:5, :]
    grad_hidden = (
        grad_result
        + scale * grad_scaled
        - hidden * (scale * scale * scale) * jnp.mean(grad_scaled * hidden, axis=-1, keepdims=True)
    )
    branch = grad_hidden.astype(jnp.bfloat16)
    da_out[...] = branch
    out_bias_grad = jnp.sum(branch.astype(jnp.float32), axis=0, keepdims=True)
    _arrive(weights, held, sems, 3)
    grad_attended = _nt(branch, held[3]).astype(jnp.bfloat16)
    first_half, masks = _head_masks(rows)
    scaling = HEAD_DIM ** (-0.5)
    for pair in range(HEADS // 2):
        lanes = slice(2 * HEAD_DIM * pair, 2 * HEAD_DIM * (pair + 1))
        query, key, value = queries_in[:, lanes], keys_in[:, lanes], values_in[:, lanes]
        grad = grad_attended[:, lanes]
        parts = []
        for mask in masks:
            scores = _nt(query * mask, key) * scaling
            shifted = jnp.exp(scores - jnp.max(scores, axis=-1, keepdims=True))
            weight = shifted / jnp.sum(shifted, axis=-1, keepdims=True)
            grad_weight = _nt(grad * mask, value)
            delta = jnp.sum(weight * grad_weight, axis=-1, keepdims=True)
            grad_score = (weight * (grad_weight - delta)).astype(jnp.bfloat16)
            parts.append(
                (
                    product(grad_score, key) * scaling,
                    _tn(grad_score, query) * scaling,
                    _tn(weight.astype(jnp.bfloat16), grad),
                )
            )
        for out, left, right in zip((dq_out, dk_out, dv_out), *parts):
            out[:, lanes] = jnp.where(first_half, left, right).astype(jnp.bfloat16)
    _arrive(weights, held, sems, 0)
    _arrive(weights, held, sems, 1)
    _arrive(weights, held, sems, 2)
    grad_first = _nt(dq_out[...], held[0]) + _nt(dk_out[...], held[1]) + _nt(dv_out[...], held[2])
    inputs = inputs_in[...].astype(jnp.float32)
    scale = rms_scale(inputs)
    attention_grad = jnp.sum(grad_first * inputs * scale, axis=0, keepdims=True)
    grad_scaled = grad_first * vectors[3:4, :]
    dx_out[...] = (
        grad_hidden
        + scale * grad_scaled
        - inputs * (scale * scale * scale) * jnp.mean(grad_scaled * inputs, axis=-1, keepdims=True)
    ).astype(jnp.bfloat16)
    small_out[0:1, :] = jnp.sum(dq_out[...].astype(jnp.float32), axis=0, keepdims=True)
    small_out[1:2, :] = jnp.sum(dv_out[...].astype(jnp.float32), axis=0, keepdims=True)
    small_out[2:3, :] = out_bias_grad
    small_out[3:4, :] = attention_grad
    small_out[4:5, :] = mixture_grad
    small_out[5:8, :] = jnp.zeros((3, feature), jnp.float32)
    small_out[5:6, :experts] = jnp.sum(onehot, axis=0, keepdims=True)
    small_out[6:7, :experts] = jnp.sum(probs, axis=0, keepdims=True)
    if later:
        grad_tokens = (next_gate[...] * dx_out[...].astype(jnp.float32)).astype(jnp.bfloat16)
        next_outgoing[...] = product(next_scatter[...], grad_tokens).astype(jnp.bfloat16)


def call(kernel, pick, arrays, weights, outs, scratch=()):
    def whole(shape):
        return pl.BlockSpec(shape, lambda i: (0,) * len(shape), pipeline_mode=pl.Buffered(1))

    anywhere = pl.BlockSpec(memory_space=pl.ANY)
    own, other = weights
    return pl.pallas_call(
        kernel,
        out_shape=[jax.ShapeDtypeStruct(shape, dtype) for shape, dtype in outs],
        grid=(1,),
        in_specs=[pl.BlockSpec(memory_space=pltpu.SMEM)]
        + [whole(array.shape) for array in arrays]
        + [anywhere] * (len(own) + len(other)),
        out_specs=[whole(shape) for shape, dtype in outs],
        scratch_shapes=[pltpu.VMEM(shape, dtype) for shape, dtype in scratch]
        + [
            pltpu.VMEM((len(own),) + own[0].shape, own[0].dtype),
            pltpu.SemaphoreType.DMA((len(own),) + own[0].shape[:-2]),
        ],
        compiler_params=pltpu.CompilerParams(vmem_limit_bytes=58 * 1024 * 1024),
    )(pick, *arrays, *own, *other)


def gelu_parts(pre):
    root = 0.7978845608028654
    square = pre * pre
    bend = jnp.tanh(root * (pre + 0.044715 * square * pre))
    slope = 0.5 * (1.0 + bend) + (0.5 * root) * pre * (1.0 - bend * bend) * (
        1.0 + 3 * 0.044715 * square
    )
    return 0.5 * pre * (1.0 + bend), slope


def sort_apart(order, mixed, rows_out, grads_out):
    group = order.shape[0]
    half = group // 2
    for i in range(mixed.shape[0] // group):
        apart = product(order[...], mixed[group * i : group * (i + 1), :]).astype(jnp.bfloat16)
        rows_out[half * i : half * (i + 1), :] = apart[:half]
        grads_out[half * i : half * (i + 1), :] = apart[half:]


def slice_kernel(
    pick_ref,
    mixed,
    order,
    own_in,
    own_down,
    other_in,
    other_down,
    rows_out,
    grads_out,
    act_out,
    grad_pre_out,
    held,
    sems,
):
    weights = ((own_in, own_down), (other_in, other_down))
    _fetch(pick_ref, weights, held, sems)
    sort_apart(order, mixed, rows_out, grads_out)
    _arrive(weights, held, sems, 0)
    act, slope = gelu_parts(product(rows_out[...], held[0]))
    act_out[...] = act.astype(jnp.bfloat16)
    _arrive(weights, held, sems, 1)
    grad_pre_out[...] = (slope * _nt(grads_out[...], held[1])).astype(jnp.bfloat16)


def _fetch_wide(pick_ref, weights, held, sems):
    for choice in (0, 1):

        @pl.when(pick_ref[0] == choice)
        def _():
            for part in range(held.shape[1]):
                for i, ref in enumerate(weights[choice]):
                    pltpu.make_async_copy(
                        ref.at[part], held.at[i, part], sems.at[i, part]
                    ).start()


def _arrive_wide(weights, held, sems, part):
    for i, ref in enumerate(weights[0]):
        pltpu.make_async_copy(ref.at[part], held.at[i, part], sems.at[i, part]).wait()


def both_ways_kernel(
    pick_ref, mixed, order, own_in, own_down, other_in, other_down, outgoing, rows, grads, held, sems
):
    weights = ((own_in, own_down), (other_in, other_down))
    _fetch_wide(pick_ref, weights, held, sems)
    sort_apart(order, mixed, rows, grads)
    total = jnp.zeros(rows.shape, jnp.float32)
    grad_total = jnp.zeros(rows.shape, jnp.float32)
    for part in range(held.shape[1]):
        _arrive_wide(weights, held, sems, part)
        act, slope = gelu_parts(product(rows[...], held[0, part]))
        total = total + product(act.astype(jnp.bfloat16), held[1, part])
        grad_pre = (slope * _nt(grads[...], held[1, part])).astype(jnp.bfloat16)
        grad_total = grad_total + _nt(grad_pre, held[0, part])
    apart = jnp.concatenate([total.astype(jnp.bfloat16), grad_total.astype(jnp.bfloat16)], axis=0)
    outgoing[...] = _tn(order[...], apart).astype(jnp.bfloat16)


def back_kernel(
    pick_ref, rows, grads, own_in, own_down, other_in, other_down, outgoing, held, sems
):
    weights = ((own_in, own_down), (other_in, other_down))
    _fetch_wide(pick_ref, weights, held, sems)
    grad_total = jnp.zeros(rows.shape, jnp.float32)
    for part in range(held.shape[1]):
        _arrive_wide(weights, held, sems, part)
        act, slope = gelu_parts(product(rows[...], held[0, part]))
        grad_pre = (slope * _nt(grads[...], held[1, part])).astype(jnp.bfloat16)
        grad_total = grad_total + _nt(grad_pre, held[0, part])
    outgoing[...] = grad_total.astype(jnp.bfloat16)


def expert_forward(rows, owned_in, owned_down):
    pre_act = product(rows, owned_in)
    activated = jax.nn.gelu(pre_act).astype(jnp.bfloat16)
    return pre_act, activated, product(activated, owned_down).astype(jnp.bfloat16)


def expert_gradients(rows, pre_act, activated, grad_rows, owned_down):
    grad_act = product(grad_rows, owned_down.T)
    grad_pre = (gelu_parts(pre_act)[1] * grad_act).astype(jnp.bfloat16)
    return product(rows.T, grad_pre), product(activated.T, grad_rows)


def in_two(tensor):
    high = lax.reduce_precision(tensor, 8, 7)
    return high.astype(jnp.bfloat16), (tensor - high).astype(jnp.bfloat16)


def dense_gradients(rows, first):
    normed, grad_queries, grad_keys, grad_values, attended, grad_branch = rows

    def pick(left, right):
        return jnp.where(first, left, right)

    own = (
        normed,
        pick(grad_queries, grad_values),
        pick(normed, attended),
        pick(grad_keys, grad_branch),
    )
    other = (
        swap(normed),
        swap(pick(grad_values, grad_queries)),
        swap(pick(attended, normed)),
        swap(pick(grad_branch, grad_keys)),
    )
    return (
        product(own[0].T, own[1]) + product(other[0].T, other[1]),
        product(own[2].T, own[3]) + product(other[2].T, other[3]),
    )


def beside(high, low):
    return jnp.concatenate([high, low, jnp.zeros_like(high)], axis=-2)


def parts_to_sum(big, small):
    devices = lax.axis_size("expert") * lax.axis_size("dp")
    feature = small.shape[1]
    share = 2 * feature // devices
    lanes = 128
    flat = small.reshape(-1)
    per_device = -(-flat.shape[0] // (devices * lanes))
    flat = jnp.pad(flat, (0, devices * per_device * lanes - flat.shape[0]))
    blocks = jnp.pad(
        flat.reshape(devices, per_device, lanes), ((0, 0), (0, 8 - per_device), (0, 0))
    )

    return jnp.concatenate(
        [
            jnp.concatenate(big).astype(jnp.bfloat16).reshape(devices, share, feature),
            beside(*in_two(blocks)),
        ],
        axis=2,
    )


def add_up(arrived):
    feature = arrived.shape[2] - 128
    arrived = jnp.sum(arrived.astype(jnp.float32), axis=0)
    sums = beside(*in_two(arrived[:8, feature:] + arrived[8:16, feature:]))
    mine = jnp.concatenate([arrived[:, :feature].astype(jnp.bfloat16), sums], axis=1)
    return mine


def sums_of(everyone, count):
    feature = everyone.shape[2] - 128
    per_device = -(-count * feature // (everyone.shape[0] * 128))
    total = everyone[:, :, :feature].reshape(2 * feature, feature)
    pairs = everyone[:, :, feature:].astype(jnp.float32)
    flat = (pairs[:, :per_device] + pairs[:, 8 : 8 + per_device]).reshape(-1)
    return total[:feature], total[feature:], flat[: count * feature].reshape(count, feature)


def on_device(
    section_ends,
    routes,
    query_weight,
    key_weight,
    value_weight,
    out_weight,
    query_bias,
    value_bias,
    out_bias,
    attention_gain,
    mixture_gain,
    router_weight,
    expert_in,
    expert_down,
):
    section_id = lax.axis_index("section")
    first = section_id == 0

    def both(own):
        return own, swap(own)

    feature = section_ends.shape[2]
    row_count = section_ends.shape[1] // MICRO
    experts = router_weight.shape[2]
    holders = lax.axis_size("dp")
    devices = lax.axis_size("expert") * holders

    def my_micro(blocks):
        blocks = blocks.reshape((MICRO, row_count) + blocks.shape[1:])
        own = lax.dynamic_index_in_dim(blocks, section_id, 0, keepdims=False)
        other = swap(lax.dynamic_index_in_dim(blocks, 1 - section_id, 0, keepdims=False))
        return jnp.where(first, own, other), jnp.where(first, other, own)

    ends = both(section_ends[0])
    route_cols = my_micro(routes[0, :, 0])
    own_weights = (query_weight[0], key_weight[0], value_weight[0], out_weight[0])
    weights = (own_weights, tuple(swap(member) for member in own_weights))
    picks = (section_id.astype(jnp.int32)[None], (1 - section_id).astype(jnp.int32)[None])
    vectors = both(
        jnp.concatenate(
            [
                query_bias,
                value_bias,
                out_bias,
                attention_gain,
                mixture_gain,
                jnp.zeros((3, feature), jnp.float32),
            ]
        )
    )
    routers = both(router_weight[0])
    onehots, codes = [], []
    position = jnp.arange(row_count)
    for col in route_cols:
        same = col[:, None] == col[None, :]
        rank = jnp.sum(same & (position[None, :] < position[:, None]), axis=1)
        codes.append(col * SLOTS + rank)
        onehots.append((col[:, None] == jnp.arange(experts)[None, :]).astype(jnp.float32))
    row = jnp.arange(devices * SLOTS)
    places0 = row // (holders * SLOTS) * SLOTS + row % SLOTS
    tokens0 = codes[0]
    row = jnp.arange(experts * BLOCK)
    apart = experts * SLOTS
    places1 = row // BLOCK * SLOTS + row % TAKEN + row % BLOCK // TAKEN * apart
    row = jnp.arange(experts * BLOCK)
    half = experts * TAKEN
    source = row % half // TAKEN * BLOCK + row % TAKEN + row // half * TAKEN
    order = (source[:, None] == row[None, :]).astype(jnp.bfloat16)
    places2 = jnp.arange(experts * SLOTS)
    tokens1 = jnp.concatenate([codes[1], codes[1] + apart])
    scatters = [
        (places[:, None] == tokens[None, :]).astype(jnp.bfloat16)
        for places, tokens in ((places0, tokens0), (places1, tokens1), (places2, tokens0))
    ]
    gathers = [
        (tokens[:, None] == places[None, :]).astype(jnp.bfloat16)
        for places, tokens in ((places0, tokens0), (places1, tokens1), (places2, tokens0))
    ]
    counts = jnp.concatenate([jnp.sum(onehot, axis=0) for onehot in onehots])
    token_total = devices * row_count
    count_row = jnp.pad(counts, (0, feature - 2 * experts))[None]

    low, full = jnp.bfloat16, jnp.float32
    block = (row_count, feature)
    kept = [
        (block, low),
        (block, low),
        (block, low),
        (block, low),
        (block, low),
        (block, full),
        (block, low),
        ((row_count, experts), full),
        ((row_count, 1), full),
    ]

    *kept0, outgoing = call(
        functools.partial(forward_kernel, False),
        picks[0],
        [*ends, count_row, onehots[0], scatters[0], *vectors, *routers],
        weights,
        kept + [((devices * SLOTS, feature), low)],
    )
    outgoing, own_in, own_down = lax.optimization_barrier(
        (outgoing, expert_in[0, 0], expert_down[0, 0])
    )
    own_experts = (own_in, own_down)
    experts_of_both = (own_experts, tuple(swap(member) for member in own_experts))
    owned_in0, owned_down0 = (
        jnp.where(first, own, other) for own, other in zip(*experts_of_both)
    )
    arrived = exchange(outgoing.reshape(devices, SLOTS, feature))
    arrived, other_in, own_down = lax.optimization_barrier(
        (arrived, experts_of_both[1][0], own_down)
    )
    early = jnp.where(first, other_in, own_down)
    late = jnp.where(first, own_down, other_in)
    early = lax.all_gather(early, "dp", axis=0)
    side = section_id.astype(jnp.int32)[None]
    shares = jnp.sum(arrived[:, -1, : 2 * experts].astype(jnp.float32), axis=0) / token_total
    shares = (shares[None, :experts], shares[None, experts:])
    rows0 = arrived.reshape(devices * SLOTS, feature)
    pre0, act0, partial = expert_forward(rows0, owned_in0, owned_down0)
    returned = exchange(partial.reshape(devices, SLOTS, feature)).reshape(-1, feature)
    returned, late = lax.optimization_barrier((returned, late))
    late = lax.all_gather(late, "dp", axis=0)

    combined0, result0, *kept1, outgoing = call(
        functools.partial(forward_kernel, True),
        picks[1],
        [
            *ends,
            kept0[5],
            kept0[8],
            gathers[0],
            returned,
            onehots[1],
            scatters[1],
            *vectors,
            *routers,
        ],
        weights,
        [(block, full), (block, low)] + kept + [((experts * BLOCK, feature), low)],
    )
    outgoing, early = lax.optimization_barrier((outgoing, early))
    early_other = swap(early)
    wide1 = ((early, early_other), (early_other, early))
    arrived = exchange_experts(outgoing)
    (outgoing,) = call(
        both_ways_kernel,
        side,
        [arrived, order],
        wide1,
        [((experts * BLOCK, feature), low)],
        [((experts * TAKEN, feature), low)] * 2,
    )
    returned = exchange_experts(outgoing)
    all_rows1 = lax.all_gather(arrived, "dp", axis=0, tiled=True)
    gradients = [
        (block, low),
        (block, low),
        (block, low),
        (block, low),
        (block, low),
        ((8 + experts, feature), full),
    ]
    result1, grad_input1, *grads1, small1, outgoing = call(
        functools.partial(backward_kernel, True),
        picks[1],
        [
            *ends,
            gathers[1],
            returned,
            result0,
            kept0[8],
            scatters[2],
            *kept1,
            onehots[1],
            shares[1],
            *vectors,
            *routers,
        ],
        weights,
        [(block, low)] + gradients + [((experts * SLOTS, feature), low)],
    )
    dense_rows1 = (kept1[0], *grads1[:3], kept1[4], grads1[3])
    parts1 = parts_to_sum(dense_gradients(dense_rows1, first), small1)

    outgoing, late = lax.optimization_barrier((outgoing, late))
    late_other = swap(late)
    wide0 = ((late_other, late), (late, late_other))
    grad_rows0 = exchange_experts(outgoing)
    rows1, grad_rows1, act1, grad_pre1 = call(
        slice_kernel,
        picks[1],
        [all_rows1, order],
        experts_of_both,
        [((devices * TAKEN, feature), low)] * 4,
    )
    in_grad1 = product(rows1.T, grad_pre1)
    down_grad1 = product(act1.T, grad_rows1)
    here = lax.dynamic_index_in_dim(
        rows0.reshape(experts, holders, SLOTS, feature),
        lax.axis_index("dp"),
        1,
        keepdims=False,
    ).reshape(-1, feature)
    (outgoing,) = call(
        back_kernel, side, [here, grad_rows0], wide0, [((experts * SLOTS, feature), low)]
    )
    returned = exchange_experts(outgoing)
    returned, parts1 = lax.optimization_barrier((returned, parts1))
    shares1 = add_up(exchange(parts1))
    gathered = lax.all_gather(grad_rows0, "dp", axis=0)
    grad_input0, *grads0, small0 = call(
        functools.partial(backward_kernel, False),
        picks[0],
        [
            *ends,
            gathers[2],
            returned,
            grad_input1,
            combined0,
            *kept0,
            onehots[0],
            shares[0],
            *vectors,
            *routers,
        ],
        weights,
        gradients,
    )
    dense_rows0 = (kept0[0], *grads0[:3], kept0[4], grads0[3])

    def own_and_other(layer0, layer1):
        own = jnp.where(first, layer0, layer1)
        return own, swap(jnp.where(first, layer1, layer0))

    def in_order(own, other):
        return jnp.where(first, jnp.stack([own, other]), jnp.stack([other, own]))

    parts0 = parts_to_sum(dense_gradients(dense_rows0, first), small0)
    parts0, shares1 = lax.optimization_barrier((parts0, shares1))
    gathered = gathered.reshape(holders, experts, SLOTS, feature).swapaxes(0, 1)
    in_grad0, down_grad0 = expert_gradients(
        rows0, pre0, act0, gathered.reshape(-1, feature), owned_down0
    )
    mine = jnp.concatenate([add_up(exchange(parts0)), shares1], axis=0)
    everyone = exchange(jnp.broadcast_to(mine[None], (devices,) + mine.shape))
    count = small0.shape[0]
    length = shares1.shape[0]
    sums0 = sums_of(everyone[:, :length], count)
    sums1 = sums_of(everyone[:, length:], count)
    own, other = [], []
    for layer0, layer1 in zip(sums0, sums1):
        pair = own_and_other(layer0, layer1)
        own.append(pair[0])
        other.append(pair[1])
    dense_sums = [
        jnp.where(first, mine, theirs).astype(jnp.float32)
        for mine, theirs in (
            (own[0], other[0]),
            (own[1], other[1]),
            (other[0], own[0]),
            (other[1], own[1]),
        )
    ]
    small = own[2] + other[2]
    statistics = in_order(own[2][5:7, :experts], other[2][5:7, :experts]) / token_total
    balances = experts * jnp.sum(statistics[:, 0] * statistics[:, 1], axis=1)

    outputs = in_order(*own_and_other(result0, result1))
    grads_in = in_order(*own_and_other(grad_input0, grad_input1))
    in_own, in_other = own_and_other(in_grad0, in_grad1)
    down_own, down_other = own_and_other(down_grad0, down_grad1)
    return (
        outputs.reshape(1, -1, feature),
        grads_in.reshape(1, -1, feature),
        balances[None],
        dense_sums[0][None],
        dense_sums[1][None],
        dense_sums[2][None],
        dense_sums[3][None],
        small[0][None],
        small[1][None],
        small[2][None],
        small[3][None],
        small[4][None],
        small[8 : 8 + experts].T[None],
        (in_own + in_other)[None, None],
        (down_own + down_other)[None, None],
    )


def solution(mesh):
    placed = (
        P("section", ("expert", "dp"), None),
        P("section", ("expert", "dp"), None),
        P("section", None, None),
        P("section", None, None),
        P("section", None, None),
        P("section", None, None),
        P("section", None),
        P("section", None),
        P("section", None),
        P("section", None),
        P("section", None),
        P("section", None, None),
        P("section", "expert", None, "dp"),
        P("section", "expert", "dp", None),
    )
    return jax.shard_map(
        on_device,
        mesh=mesh,
        in_specs=placed,
        out_specs=(
            P("section", ("expert", "dp"), None),
            P("section", ("expert", "dp"), None),
            P("section", None),
            P("section", None, None),
            P("section", None, None),
            P("section", None, None),
            P("section", None, None),
            P("section", None),
            P("section", None),
            P("section", None),
            P("section", None),
            P("section", None),
            P("section", None, None),
            P("section", "expert", None, "dp"),
            P("section", "expert", "dp", None),
        ),
        check_vma=False,
    )
```
